32 devices in a mesh: gx: 8 (over z, x), gy: 4 (over y, core).
Axes of the slice: x: 2, y: 2, z: 4, core: 2. Of those that a mesh axis runs over, the one named last changes fastest.
Arguments:
- eigen: float32 [256, 256, 256], P('gx', 'gy'), may hold values from -6 to 6
- seg_vec: float32 [6, 8, 4, 2048], P(None, 'gx', 'gy'), may hold values from -5 to 5
- seg_off: float32 [3, 8, 4, 2048], P(None, 'gx', 'gy'), may hold values from 0 to 1
- seg_cell: int32 [8, 4, 2048], P('gx', 'gy'), may hold values from 0 to 524287
- blk_count: int32 [8, 4, 16], P('gx', 'gy'), may hold values from 0 to 128, as said below
- pair_list: int32 [8, 4, 16, 8], P('gx', 'gy'), may hold values from 0 to 143, as said below
Outputs:
- stress_field: float32 [256, 256, 256], P('gx', 'gy')
- seg_force: float32 [3, 8, 4, 2048], P(None, 'gx', 'gy')
The draws below stay inside these ranges and needn't reach their ends.
Inputs may be any that keep to these rules, and one draw needn't show every extreme that they name: `blk_count`: A block's live segments fill its first slots; at least one device holds 16 full blocks of 128; every device holds a block with segments. `pair_list`: the 8 entries of one block are distinct.
All inputs are finite; a program needn't handle non-finite values.
Results may differ from the reference program's by a relative error of at most 0.0003.
Values sent between devices are 32-bit elements; how exact they have to be, the bound alone decides.
No kernel may reach another device: no remote copies, remote signals or barrier semaphores. Data moves between devices by JAX's collectives and lax.ppermute only.
A program may use at most 64 MiB of HBM per device.

```python
import math
import jax
import jax.numpy as jnp
from jax import lax

GRID = 256
SEGS_BLK = 128
BLK_DEV = 16
PARTNERS = 8
SEG_DEV = 2048
CELLS_DEV = 524288
N_GX = 8
N_GY = 4


def draw_eigen(key, part):
    first = jax.random.fold_in(key, 0)
    field = jax.random.normal(first, (GRID, GRID, GRID), jnp.float32)
    return jnp.clip(field, -6.0, 6.0)


def draw_blk_count(key, part):
    key_list = jax.random.split(key, 4)
    devices = N_GX * N_GY
    tangled = jax.random.randint(key_list[0], (devices,), 0, 8) == 0
    chosen = jax.random.randint(key_list[1], (), 0, devices)
    tangled = tangled | (jnp.arange(devices, dtype=jnp.int32) == chosen)
    live_blocks = jax.random.randint(key_list[2], (devices,), 1, max(BLK_DEV // 2, 1) + 1)
    live_blocks = jnp.where(tangled, BLK_DEV, live_blocks)
    filled = jax.random.randint(key_list[3], (devices, BLK_DEV), SEGS_BLK // 4, SEGS_BLK + 1)
    filled = jnp.where(tangled[:, None], SEGS_BLK, filled)
    result = jnp.where(jnp.arange(BLK_DEV, dtype=jnp.int32)[None, :] < live_blocks[:, None], filled, 0)
    return result.astype(jnp.int32).reshape(N_GX, N_GY, BLK_DEV)


def draw_pair_list(key, part):
    row_total = N_GX * N_GY * BLK_DEV
    pool_size = 9 * BLK_DEV
    scores = jax.random.randint(key, (row_total, pool_size), 0, 1 << 20)
    scores = scores * pool_size + jnp.arange(pool_size, dtype=jnp.int32)[None, :]
    ranking = jnp.argsort(scores, axis=1)
    return ranking[:, :PARTNERS].astype(jnp.int32).reshape(N_GX, N_GY, BLK_DEV, PARTNERS)


def touch_ends(entries, stream_key, smallest, largest):
    dims = entries.shape
    spot = [jax.random.randint(jax.random.fold_in(stream_key, axis), (), 0, dims[axis]) for axis in range(len(dims))]
    entries = entries.at[tuple(spot)].set(smallest)
    longest = dims.index(max(dims))
    spot[longest] = (spot[longest] + 1) % dims[longest]
    return entries.at[tuple(spot)].set(largest)


def steps_of(rng, extent, pieces, least, largest):
    level = 1.0
    for dim, shards_of in pieces:
        draws = jax.random.uniform(jax.random.fold_in(jax.random.fold_in(rng, 6), dim), (shards_of,), jnp.float32, least / len(pieces), largest / len(pieces))
        level = level * jnp.repeat(jnp.exp(draws), extent[dim] // shards_of).reshape((-1,) + (1,) * (len(extent) - 1 - dim))
    return level


def gaussian(own_key, shape, scale, bound, cuts=(), kind=jnp.bfloat16):
    values = scale * jax.random.normal(own_key, shape, jnp.float32)
    if cuts:
        values = values * steps_of(own_key, shape, cuts, -0.22, 0.18)
    return jnp.clip(values, -bound, bound).astype(kind)


def setup_inputs(seed: int = 0) -> dict:
    key_of = jax.random.split(jax.random.key(seed), 7)
    eigen = draw_eigen(jax.random.fold_in(key_of[6], 71), 0)
    seg_vec = gaussian(key_of[1], (6, N_GX, N_GY, SEG_DEV), 1.0, 5.0, ((1, 8), (2, 4)), jnp.float32)
    seg_off = jnp.clip(1.0 * jax.random.uniform(key_of[2], (3, N_GX, N_GY, SEG_DEV), jnp.float32) ** steps_of(key_of[2], (3, N_GX, N_GY, SEG_DEV), ((1, 8), (2, 4)), -0.2, 0.2), 0.0, 1.0)
    seg_cell = touch_ends(jax.random.randint(key_of[3], (N_GX, N_GY, SEG_DEV), 0, CELLS_DEV), jax.random.fold_in(key_of[3], 1), 0, CELLS_DEV - 1).astype(jnp.int32)
    blk_count = draw_blk_count(jax.random.fold_in(key_of[6], 71), 0)
    pair_list = draw_pair_list(jax.random.fold_in(key_of[6], 71), 0)
    return {"eigen": eigen, "seg_vec": seg_vec, "seg_off": seg_off, "seg_cell": seg_cell, "blk_count": blk_count, "pair_list": pair_list}


nu_copper = 0.34
core_sq = 4.0
pair_scale = 4.0

def wave_sq(freq, length):
    sine = 2.0 * jnp.sin(math.pi * freq.astype(jnp.float32) / length)
    return sine * sine

def multiplier(wave_x, wave_y, wave_z, anchor):
    total = wave_x + wave_y + wave_z
    safe = jnp.where(anchor, 1.0, total)
    return -2.0 * (1.0 - (wave_x + wave_z) / safe + 2.0 * wave_x * wave_z / ((1.0 - nu_copper) * safe * safe))

def block_force(own_data, far_data, tau_own):
    deltas = [own_data[k][:, None] - far_data[k][None, :] for k in range(3)]
    dist_sq = deltas[0] * deltas[0] + deltas[1] * deltas[1] + deltas[2] * deltas[2] + core_sq
    inverse = 1.0 / jnp.sqrt(dist_sq)
    inv_three = inverse * inverse * inverse
    inv_five = inv_three * inverse * inverse
    burg_dot = own_data[3][:, None] * far_data[3][None, :] + own_data[4][:, None] * far_data[4][None, :] + own_data[5][:, None] * far_data[5][None, :]
    line_dot = own_data[6][:, None] * far_data[6][None, :] + own_data[7][:, None] * far_data[7][None, :] + own_data[8][:, None] * far_data[8][None, :]
    burg_own = own_data[3][:, None] * deltas[0] + own_data[4][:, None] * deltas[1] + own_data[5][:, None] * deltas[2]
    burg_far = far_data[3][None, :] * deltas[0] + far_data[4][None, :] * deltas[1] + far_data[5][None, :] * deltas[2]
    weight = line_dot * (burg_dot * inv_three - 3.0 * burg_own * burg_far * inv_five)
    pair_pull = jnp.stack([lax.optimization_barrier(jnp.sum(weight * deltas[k], axis=1)) for k in range(3)])
    burgers = own_data[3:6]
    tangent = own_data[6:9]
    glide_dir = jnp.stack([burgers[1] * tangent[2] - burgers[2] * tangent[1], burgers[2] * tangent[0] - burgers[0] * tangent[2], burgers[0] * tangent[1] - burgers[1] * tangent[0]])
    return pair_scale * pair_pull + tau_own[None, :] * glide_dir

def reference(eigen, seg_vec, seg_off, seg_cell, blk_count, pair_list):
    freq = jnp.arange(GRID, dtype=jnp.int32)
    wave = wave_sq(freq, GRID)
    anchor = (freq[:, None, None] == 0) & (freq[None, :, None] == 0) & (freq[None, None, :] == 0)
    gain = multiplier(wave[:, None, None], wave[None, :, None], wave[None, None, :], anchor)
    stress = jnp.real(jnp.fft.ifftn(jnp.fft.fftn(eigen) * gain)).astype(jnp.float32)
    plane_x = GRID // N_GX
    plane_y = GRID // N_GY
    blocks = stress.reshape(N_GX, plane_x, N_GY, plane_y, GRID).transpose(0, 2, 1, 3, 4).reshape(N_GX, N_GY, plane_x * plane_y * GRID)
    sampled = jnp.take_along_axis(blocks, seg_cell, axis=2)
    coord_z = seg_cell % GRID
    coord_y = seg_cell // GRID % plane_y
    coord_x = seg_cell // (GRID * plane_y)
    position = jnp.stack([coord_x, coord_y, coord_z]).astype(jnp.float32) + seg_off
    live = (jnp.arange(SEGS_BLK, dtype=jnp.int32)[None, None, None, :] < blk_count[..., None]).reshape(N_GX, N_GY, SEG_DEV).astype(jnp.float32)
    source = jnp.concatenate([position, seg_vec[0:3] * live[None], seg_vec[3:6]], axis=0)
    shift = (jnp.arange(3, dtype=jnp.int32) - 1).astype(jnp.float32)

    def device(device_id):
        row_id = device_id // N_GY
        col_id = device_id % N_GY
        row_ids = ((row_id + jnp.arange(3, dtype=jnp.int32) - 1) % N_GX).astype(jnp.int32)
        col_ids = ((col_id + jnp.arange(3, dtype=jnp.int32) - 1) % N_GY).astype(jnp.int32)
        nearby = source[:, row_ids][:, :, col_ids]
        nearby = nearby.at[0].add(shift[:, None, None] * plane_x).at[1].add(shift[None, :, None] * plane_y)
        source_pool = nearby.reshape(9, 9 * BLK_DEV, SEGS_BLK)
        own_blocks = source[:, row_id, col_id].reshape(9, BLK_DEV, SEGS_BLK).transpose(1, 0, 2)
        tau_blocks = sampled[row_id, col_id].reshape(BLK_DEV, SEGS_BLK)

        def one_block(inputs):
            own_data, partner_ids, tau_own = inputs
            far_data = source_pool[:, partner_ids].reshape(9, -1)
            return block_force(own_data, far_data, tau_own)
        return lax.map(one_block, (own_blocks, pair_list[row_id, col_id], tau_blocks))
    forces = lax.map(device, jnp.arange(N_GX * N_GY, dtype=jnp.int32))
    seg_force = forces.reshape(N_GX, N_GY, BLK_DEV, 3, SEGS_BLK).transpose(3, 0, 1, 2, 4).reshape(3, N_GX, N_GY, SEG_DEV)
    return (stress, seg_force)
```

```python
import math

import jax
import jax.numpy as jnp
import numpy as np
from jax import lax
from jax.experimental import pallas as pl
from jax.experimental.pallas import tpu as pltpu
from jax.sharding import PartitionSpec as P

nu_copper = 0.34
core_sq = 4.0
pair_scale = 4.0
CHUNKS = 2
VMEM_LIMIT = 48 * 1024 * 1024


def hartley_table(length):
    phase = np.outer(np.arange(length), np.arange(length)) % length
    angle = phase * (2.0 * math.pi / length)
    return ((np.cos(angle) + np.sin(angle)) / math.sqrt(length)).astype(np.float32)


def line_tables(length, plane_x):
    freq = np.arange(length, dtype=np.float64)
    wave = (2.0 * np.sin(math.pi * freq / length)) ** 2
    wave_z = wave[:, None]
    wave_y = wave[None, :]
    total = wave_y + wave_z
    zero = total == 0.0
    safe = np.where(zero, 1.0, total)
    ratio = 1.0 / (1.0 + safe / 2.0 + np.sqrt(safe + safe * safe / 4.0))
    ratio = ratio.astype(np.float32).astype(np.float64)
    elastic = 2.0 / (1.0 - nu_copper)
    gap = 1.0 - ratio * ratio
    green = ratio / gap
    first = -2.0 * (wave_y + elastic * wave_z) * green
    second = 2.0 * elastic * wave_z * safe * green * green
    weight_two = second
    weight_one = first + second * 2.0 * ratio * ratio / gap
    weight_zero = -first - second * (1.0 + ratio * ratio) / gap
    lap = ratio**length
    wrap_one = 1.0 / (1.0 - lap)
    wrap_two = length * lap / (1.0 - lap) ** 2
    leap = ratio**plane_x
    mask = np.where(zero, 0.0, 1.0)
    ratio = np.where(zero, 1.0, ratio)
    leap = np.where(zero, 1.0, leap)
    weight_zero = np.where(zero, 0.0, weight_zero)
    weight_one = np.where(zero, -1.0 / length, weight_one)
    weight_two = np.where(zero, 0.0, weight_two)
    wrap_one = np.where(zero, 1.0, wrap_one)
    wrap_two = np.where(zero, 0.0, wrap_two)
    tables = [ratio, leap, mask, weight_zero, weight_one, weight_two, wrap_one, wrap_two]
    return np.stack([t.astype(np.float32) for t in tables])


def halves(value):
    high = value.astype(jnp.bfloat16)
    low = (value - high.astype(jnp.float32)).astype(jnp.bfloat16)
    return high, low


def three_dots(left, right, dims):
    def one(a, b):
        return lax.dot_general(a, b, (dims, ((), ())), preferred_element_type=jnp.float32)

    return one(left[0], right[0]) + one(left[0], right[1]) + one(left[1], right[0])


def whole(memory=pltpu.VMEM):
    return pl.BlockSpec(memory_space=memory)


def params():
    return pltpu.CompilerParams(vmem_limit_bytes=VMEM_LIMIT)


def z_forward(field, table, me, groups, chunk, rows):
    cells, length = field.shape
    per = length // groups
    tile = min(512, cells)

    def kernel(me_ref, field_ref, table_ref, *outs):
        own = me_ref[0]
        picked = [
            table_ref[pl.ds(pl.multiple_of((own ^ d) * per + chunk * rows, 8), rows), :]
            for d in range(groups)
        ]
        left = halves(jnp.concatenate(picked, axis=0))
        right = halves(field_ref[...])
        result = three_dots(left, right, ((1,), (1,)))
        for d in range(groups):
            outs[d][...] = result[d * rows : (d + 1) * rows]

    return pl.pallas_call(
        kernel,
        grid=(cells // tile,),
        in_specs=[
            pl.BlockSpec(memory_space=pltpu.SMEM),
            pl.BlockSpec((tile, length), lambda i: (i, 0)),
            pl.BlockSpec((length, length), lambda i: (0, 0)),
        ],
        out_specs=[pl.BlockSpec((rows, tile), lambda i: (0, i))] * groups,
        out_shape=[jax.ShapeDtypeStruct((rows, cells), jnp.float32)] * groups,
        compiler_params=params(),
        cost_estimate=pl.CostEstimate(
            flops=6 * cells * length * rows * groups, bytes_accessed=8 * cells * length, transcendentals=0
        ),
        name="z_forward",
    )(me, field, table)


def y_rows(table_ref, own, groups, plane_y):
    picked = [
        table_ref[pl.ds(pl.multiple_of((own ^ d) * plane_y, 8), plane_y), :] for d in range(groups)
    ]
    return halves(jnp.concatenate(picked, axis=0))


def y_forward(parts, table, lines, me, chunk, rows, plane_x, plane_y):
    groups = len(parts)
    length = table.shape[0]
    per = length // groups

    def kernel(me_ref, *refs):
        part_refs = refs[:groups]
        table_ref, lines_ref, spec_ref, ends_ref, gathered = refs[groups:]
        own = me_ref[0]
        right = y_rows(table_ref, own, groups, plane_y)
        for x in range(plane_x):
            gathered[x * rows : (x + 1) * rows, :] = jnp.concatenate(
                [ref[:, x * plane_y : (x + 1) * plane_y] for ref in part_refs], axis=1
            )
        result = three_dots(halves(gathered[...]), right, ((1,), (0,)))
        gathered[...] = result
        first = pl.multiple_of(own * per + chunk * rows, 8)
        ratio = lines_ref[0, pl.ds(first, rows), :]
        mask = lines_ref[2, pl.ds(first, rows), :]
        for g in range(0, rows, 8):
            step = ratio[g : g + 8]
            keep = mask[g : g + 8]
            zero = jnp.zeros_like(step)
            one, two = zero, zero
            for x in range(plane_x):
                value = gathered[x * rows + g : x * rows + g + 8, :]
                one = value + step * one
                two = one + step * two
                spec_ref[x, g : g + 8, :] = value * keep
            ends_ref[0, g : g + 8, :] = one
            ends_ref[1, g : g + 8, :] = two
            one, two = zero, zero
            for x in reversed(range(plane_x)):
                value = gathered[x * rows + g : x * rows + g + 8, :]
                one = value + step * one
                two = one + step * two
            ends_ref[2, g : g + 8, :] = one
            ends_ref[3, g : g + 8, :] = two

    return pl.pallas_call(
        kernel,
        in_specs=[whole(pltpu.SMEM)] + [whole()] * (groups + 2),
        out_specs=[whole(), whole()],
        out_shape=[
            jax.ShapeDtypeStruct((plane_x, rows, length), jnp.float32),
            jax.ShapeDtypeStruct((4, rows, length), jnp.float32),
        ],
        scratch_shapes=[pltpu.VMEM((plane_x * rows, length), jnp.float32)],
        compiler_params=params(),
        cost_estimate=pl.CostEstimate(
            flops=6 * plane_x * rows * length * length,
            bytes_accessed=8 * plane_x * rows * length,
            transcendentals=0,
        ),
        name="y_forward",
    )(me, *parts, table, lines)


def y_backward(spec, ends, table, lines, me, chunk, groups, plane_y):
    plane_x, rows, length = spec.shape
    per = length // groups
    blocks = len(ends)

    def kernel(me_ref, spec_ref, *refs):
        ends_refs = refs[:blocks]
        table_ref, lines_ref = refs[blocks : blocks + 2]
        outs = refs[blocks + 2 : blocks + 2 + groups]
        work = refs[blocks + 2 + groups]
        own = me_ref[0]
        right = y_rows(table_ref, own, groups, plane_y)
        first = pl.multiple_of(own * per + chunk * rows, 8)
        for g in range(0, rows, 8):
            at = pl.ds(pl.multiple_of(first + g, 8), 8)
            step, leap = lines_ref[0, at, :], lines_ref[1, at, :]
            wrap_one, wrap_two = lines_ref[6, at, :], lines_ref[7, at, :]
            carries = []
            for side in (0, 1):
                one = jnp.zeros_like(step)
                two = jnp.zeros_like(step)
                for distance in reversed(range(1, blocks + 1)):
                    source = distance % blocks if side == 0 else (blocks - distance) % blocks
                    ref = ends_refs[source]
                    two = ref[2 * side + 1, g : g + 8, :] + leap * (two + float(plane_x) * one)
                    one = ref[2 * side, g : g + 8, :] + leap * one
                carries.append((one * wrap_one, two * wrap_one + wrap_two * one))
            weight_zero, weight_one, weight_two = lines_ref[3, at, :], lines_ref[4, at, :], lines_ref[5, at, :]
            one, two = carries[0]
            for x in range(plane_x):
                value = spec_ref[x, g : g + 8, :]
                one = value + step * one
                two = one + step * two
                work[x * rows + g : x * rows + g + 8, :] = (
                    weight_zero * value + weight_one * one + weight_two * two
                )
            one, two = carries[1]
            for x in reversed(range(plane_x)):
                value = spec_ref[x, g : g + 8, :]
                one = value + step * one
                two = one + step * two
                work[x * rows + g : x * rows + g + 8, :] += weight_one * one + weight_two * two
        work[...] = three_dots(halves(work[...]), right, ((1,), (1,)))
        pack = max(1, 128 // plane_y)
        for x in range(0, plane_x, pack):
            for d in range(groups):
                outs[d][:, x * plane_y : (x + pack) * plane_y] = jnp.concatenate(
                    [
                        work[(x + k) * rows : (x + k + 1) * rows, d * plane_y : (d + 1) * plane_y]
                        for k in range(pack)
                    ],
                    axis=1,
                )

    return pl.pallas_call(
        kernel,
        in_specs=[whole(pltpu.SMEM)] + [whole()] * (blocks + 3),
        out_specs=[whole()] * groups,
        out_shape=[jax.ShapeDtypeStruct((rows, plane_x * plane_y), jnp.float32)] * groups,
        scratch_shapes=[pltpu.VMEM((plane_x * rows, length), jnp.float32)],
        compiler_params=params(),
        cost_estimate=pl.CostEstimate(
            flops=6 * plane_x * rows * length * length,
            bytes_accessed=8 * plane_x * rows * length,
            transcendentals=0,
        ),
        name="y_backward",
    )(me, spec, *ends, table, lines)


def z_backward(parts, table, cells, pull, vectors, me, groups, chunks, rows):
    cell_total = parts[0].shape[1]
    length = table.shape[0]
    per = length // groups
    seg_total = cells.shape[1]
    blocks, width = pull.shape[1:]
    tile = min(512, cell_total)
    steps = cell_total // tile

    def kernel(me_ref, *refs):
        part_refs = refs[: chunks * groups]
        table_ref, cells_ref, pull_ref, vectors_ref, stress_ref, force_ref, samples = refs[chunks * groups :]
        own = me_ref[0]
        i = pl.program_id(0)
        picked = [
            table_ref[pl.ds(pl.multiple_of((own ^ d) * per + c * rows, 8), rows), :]
            for c in range(chunks)
            for d in range(groups)
        ]
        picked = jnp.concatenate(picked, axis=0)
        right = halves(picked)
        stack = jnp.concatenate([ref[...] for ref in part_refs], axis=0)
        left = halves(stack)
        stress_ref[...] = three_dots(left, right, ((0,), (0,)))
        place = cells_ref[...] // length - i * tile
        hot = (lax.broadcasted_iota(jnp.int32, (tile, seg_total), 0) == place).astype(jnp.bfloat16)
        found = jnp.dot(left[0], hot, preferred_element_type=jnp.float32) + jnp.dot(
            left[1], hot, preferred_element_type=jnp.float32
        )

        @pl.when(i == 0)
        def _():
            samples[...] = found

        @pl.when(i > 0)
        def _():
            samples[...] += found

        @pl.when(i == steps - 1)
        def _():
            depth = cells_ref[...] % length
            hot_z = (lax.broadcasted_iota(jnp.int32, (length, seg_total), 0) == depth).astype(jnp.bfloat16)
            factor = jnp.dot(right[0], hot_z, preferred_element_type=jnp.float32) + jnp.dot(
                right[1], hot_z, preferred_element_type=jnp.float32
            )
            tau = jnp.sum(samples[...] * factor, axis=0, keepdims=True)
            tau = jnp.concatenate([tau[:, b * width : (b + 1) * width] for b in range(blocks)], axis=0)
            b0, b1, b2, t0, t1, t2 = (vectors_ref[k] for k in range(6))
            force_ref[0] = pull_ref[0] + tau * (b1 * t2 - b2 * t1)
            force_ref[1] = pull_ref[1] + tau * (b2 * t0 - b0 * t2)
            force_ref[2] = pull_ref[2] + tau * (b0 * t1 - b1 * t0)

    return pl.pallas_call(
        kernel,
        grid=(steps,),
        in_specs=[whole(pltpu.SMEM)]
        + [pl.BlockSpec((rows, tile), lambda i: (0, i))] * (chunks * groups)
        + [
            pl.BlockSpec((length, length), lambda i: (0, 0)),
            pl.BlockSpec((1, seg_total), lambda i: (0, 0)),
            pl.BlockSpec((3, blocks, width), lambda i: (0, 0, 0)),
            pl.BlockSpec((6, blocks, width), lambda i: (0, 0, 0)),
        ],
        out_specs=[
            pl.BlockSpec((tile, length), lambda i: (i, 0)),
            pl.BlockSpec((3, blocks, width), lambda i: (0, 0, 0)),
        ],
        out_shape=[
            jax.ShapeDtypeStruct((cell_total, length), jnp.float32),
            jax.ShapeDtypeStruct((3, blocks, width), jnp.float32),
        ],
        scratch_shapes=[pltpu.VMEM((length, seg_total), jnp.float32)],
        compiler_params=params(),
        cost_estimate=pl.CostEstimate(
            flops=10 * cell_total * length * length, bytes_accessed=8 * cell_total * length, transcendentals=0
        ),
        name="z_backward",
    )(me, *parts, table, cells, pull, vectors)


def pair_pull(pool, pairs, lively, shifts, first, count):
    devices = len(pool)
    rows, blocks, width = pool[0].shape
    partners = pairs.shape[1]

    def kernel(pairs_ref, lively_ref, *refs):
        pool_refs = refs[:devices]
        out_ref, far, near, total = refs[devices:]
        for d in range(devices):
            for k in range(rows):
                value = pool_refs[d][k]
                if k < 2 and shifts[d][k] != 0.0:
                    value = value + shifts[d][k]
                far[(d * rows + k) * blocks : (d * rows + k + 1) * blocks, :] = value
        home = devices // 2 * rows * blocks

        def one_block(index, carry):
            b = first + index
            own = [far[pl.ds(home + k * blocks + b, 1), :] for k in range(rows)]
            own = jnp.concatenate(own + [jnp.zeros((16 - rows, width), jnp.float32)], axis=0)
            own = own.T
            for k in range(rows):
                near[k] = jnp.broadcast_to(own[:, k : k + 1], (width, width))
            total[...] = jnp.zeros_like(total)

            def one_partner(p, carry):
                number = pairs_ref[b, p]

                @pl.when(lively_ref[number] > 0)
                def _():
                    base = (number // blocks) * (rows * blocks) + number % blocks
                    other = [
                        jnp.broadcast_to(far[pl.ds(base + k * blocks, 1), :], (8, width)) for k in range(rows)
                    ]
                    for t in range(0, width, 8):
                        mine = [near[k, t : t + 8, :] for k in range(rows)]
                        dx, dy, dz = (mine[k] - other[k] for k in range(3))
                        inverse = lax.rsqrt(dx * dx + dy * dy + dz * dz + core_sq)
                        squared = inverse * inverse
                        burg_dot = mine[3] * other[3] + mine[4] * other[4] + mine[5] * other[5]
                        line_dot = mine[6] * other[6] + mine[7] * other[7] + mine[8] * other[8]
                        burg_own = mine[3] * dx + mine[4] * dy + mine[5] * dz
                        burg_far = other[3] * dx + other[4] * dy + other[5] * dz
                        weight = (line_dot * (squared * inverse)) * (
                            burg_dot - (3.0 * squared) * (burg_own * burg_far)
                        )
                        total[0, t : t + 8, :] += weight * dx
                        total[1, t : t + 8, :] += weight * dy
                        total[2, t : t + 8, :] += weight * dz

                return carry

            lax.fori_loop(0, partners, one_partner, 0)
            for k in range(3):
                summed = jnp.sum(total[k].T, axis=0, keepdims=True)
                out_ref[k, pl.ds(index, 1), :] = pair_scale * summed
            return carry

        lax.fori_loop(0, count, one_block, 0)

    return pl.pallas_call(
        kernel,
        in_specs=[whole(pltpu.SMEM)] * 2 + [whole()] * devices,
        out_specs=whole(),
        out_shape=jax.ShapeDtypeStruct((3, count, width), jnp.float32),
        scratch_shapes=[
            pltpu.VMEM((devices * rows * blocks, width), jnp.float32),
            pltpu.VMEM((rows, width, width), jnp.float32),
            pltpu.VMEM((3, width, width), jnp.float32),
        ],
        compiler_params=params(),
        cost_estimate=pl.CostEstimate(
            flops=50 * count * partners * width * width,
            bytes_accessed=4 * devices * rows * blocks * width,
            transcendentals=count * partners * width * width,
        ),
        name="pair_pull",
    )(pairs, lively, *pool)


def per_device(eigen, seg_vec, seg_off, seg_cell, blk_count, pair_list):
    plane_x, plane_y, length = eigen.shape
    groups_x = lax.axis_size("gx")
    groups_y = lax.axis_size("gy")
    per = length // groups_y
    chunks = CHUNKS if per // CHUNKS >= 8 else 1
    rows = per // chunks
    me = lax.axis_index("gy").astype(jnp.int32).reshape(1)
    table = jnp.asarray(hartley_table(length))
    lines = jnp.asarray(line_tables(length, plane_x))

    seg_total = seg_cell.shape[2]
    block_total = blk_count.shape[2]
    width = seg_total // block_total
    cells = seg_cell.reshape(block_total, width)
    vectors = seg_vec.reshape(6, block_total, width)
    position = jnp.stack(
        [cells // (length * plane_y), cells // length % plane_y, cells % length]
    ).astype(jnp.float32) + seg_off.reshape(3, block_total, width)
    counts = blk_count.reshape(block_total)
    live = (jnp.arange(width, dtype=jnp.int32)[None, :] < counts[:, None]).astype(jnp.float32)
    live_vectors = jnp.concatenate([vectors[0:3] * live[None], vectors[3:6]], axis=0)
    source = jnp.concatenate([position, live_vectors], axis=0)

    field = eigen.reshape(plane_x * plane_y, length)
    sent = [z_forward(field, table, me, groups_y, c, rows) for c in range(chunks)]

    def swap(parts):
        return [parts[0]] + [
            lax.ppermute(parts[d], "gy", [(i, i ^ d) for i in range(groups_y)])
            for d in range(1, groups_y)
        ]

    arrived = [swap(parts) for parts in sent]

    pool, shifts = [], []
    for p in (-1, 0, 1):
        for q in (-1, 0, 1):
            shifts.append((float(p * plane_x), float(q * plane_y)))
            if p == 0 and q == 0:
                pool.append(source)
                continue
            route = [
                (((i + p) % groups_x) * groups_y + (j + q) % groups_y, i * groups_y + j)
                for i in range(groups_x)
                for j in range(groups_y)
            ]
            pool.append(lax.ppermute(source, ("gx", "gy"), route))
    lively = jnp.concatenate([jnp.any(part[3:6] != 0.0, axis=(0, 2)) for part in pool]).astype(jnp.int32)
    pairs = pair_list.reshape(block_total, pair_list.shape[3])
    pull = pair_pull(pool, pairs, lively, shifts, 0, block_total)

    returned = []
    for c in range(chunks):
        spec, ends = y_forward(arrived[c], table, lines, me, c, rows, plane_x, plane_y)
        all_ends = [ends] + [
            lax.ppermute(ends, "gx", [(i, (i + e) % groups_x) for i in range(groups_x)])
            for e in range(1, groups_x)
        ]
        returned.append(y_backward(spec, all_ends, table, lines, me, c, groups_y, plane_y))
    landed = [swap(parts) for parts in returned]
    flat = [part for parts in landed for part in parts]
    stress, force = z_backward(
        flat, table, seg_cell.reshape(1, seg_total), pull, live_vectors, me, groups_y, chunks, rows
    )
    return stress.reshape(eigen.shape), force.reshape(3, 1, 1, seg_total)


def solution(mesh):
    return jax.shard_map(
        per_device,
        mesh=mesh,
        in_specs=(
            P("gx", "gy", None),
            P(None, "gx", "gy", None),
            P(None, "gx", "gy", None),
            P("gx", "gy", None),
            P("gx", "gy", None),
            P("gx", "gy", None, None),
        ),
        out_specs=(P("gx", "gy", None), P(None, "gx", "gy", None)),
        check_vma=False,
    )
```

```python
import math

import jax
import jax.numpy as jnp
import numpy as np
from jax import lax
from jax.experimental import pallas as pl
from jax.experimental.pallas import tpu as pltpu
from jax.sharding import PartitionSpec as P

nu_copper = 0.34
core_sq = 4.0
pair_scale = 4.0
CHUNKS = 2
VMEM_LIMIT = 24 * 1024 * 1024


def hartley_table(length):
    phase = np.outer(np.arange(length), np.arange(length)) % length
    angle = phase * (2.0 * math.pi / length)
    return ((np.cos(angle) + np.sin(angle)) / math.sqrt(length)).astype(np.float32)


def line_tables(length, plane_x):
    freq = np.arange(length, dtype=np.float64)
    wave = (2.0 * np.sin(math.pi * freq / length)) ** 2
    wave_z = wave[:, None]
    wave_y = wave[None, :]
    total = wave_y + wave_z
    zero = total == 0.0
    safe = np.where(zero, 1.0, total)
    ratio = 1.0 / (1.0 + safe / 2.0 + np.sqrt(safe + safe * safe / 4.0))
    ratio = ratio.astype(np.float32).astype(np.float64)
    elastic = 2.0 / (1.0 - nu_copper)
    gap = 1.0 - ratio * ratio
    green = ratio / gap
    first = -2.0 * (wave_y + elastic * wave_z) * green
    second = 2.0 * elastic * wave_z * safe * green * green
    weight_two = second
    weight_one = first + second * 2.0 * ratio * ratio / gap
    weight_zero = -first - second * (1.0 + ratio * ratio) / gap
    lap = ratio**length
    wrap_one = 1.0 / (1.0 - lap)
    wrap_two = length * lap / (1.0 - lap) ** 2
    leap = ratio**plane_x
    mask = np.where(zero, 0.0, 1.0)
    ratio = np.where(zero, 1.0, ratio)
    leap = np.where(zero, 1.0, leap)
    weight_zero = np.where(zero, 0.0, weight_zero)
    weight_one = np.where(zero, -1.0 / length, weight_one)
    weight_two = np.where(zero, 0.0, weight_two)
    wrap_one = np.where(zero, 1.0, wrap_one)
    wrap_two = np.where(zero, 0.0, wrap_two)
    tables = [ratio, leap, mask, weight_zero, weight_one, weight_two, wrap_one, wrap_two]
    return np.stack([t.astype(np.float32) for t in tables])


def halves(value):
    high = value.astype(jnp.bfloat16)
    low = (value - high.astype(jnp.float32)).astype(jnp.bfloat16)
    return high, low


def three_dots(left, right, dims):
    def one(a, b):
        return lax.dot_general(a, b, (dims, ((), ())), preferred_element_type=jnp.float32)

    return one(left[0], right[0]) + one(left[0], right[1]) + one(left[1], right[0])


def whole(memory=pltpu.VMEM):
    return pl.BlockSpec(memory_space=memory)


def anywhere(count):
    return [pl.BlockSpec(memory_space=pl.ANY)] * count


def params():
    return pltpu.CompilerParams(vmem_limit_bytes=VMEM_LIMIT)


def z_forward(field, table, me, groups, chunk, rows, after):
    cells, length = field.shape
    per = length // groups
    tile = min(512, cells)

    def kernel(me_ref, field_ref, table_ref, *refs):
        outs = refs[-groups:]
        own = me_ref[0]
        picked = [
            table_ref[pl.ds(pl.multiple_of((own ^ d) * per + chunk * rows, 8), rows), :]
            for d in range(groups)
        ]
        left = halves(jnp.concatenate(picked, axis=0))
        right = halves(field_ref[...])
        result = three_dots(left, right, ((1,), (1,)))
        for d in range(groups):
            outs[d][...] = result[d * rows : (d + 1) * rows]

    return pl.pallas_call(
        kernel,
        grid=(cells // tile,),
        in_specs=[
            pl.BlockSpec(memory_space=pltpu.SMEM),
            pl.BlockSpec((tile, length), lambda i: (i, 0)),
            pl.BlockSpec((length, length), lambda i: (0, 0)),
        ]
        + anywhere(len(after)),
        out_specs=[pl.BlockSpec((rows, tile), lambda i: (0, i))] * groups,
        out_shape=[jax.ShapeDtypeStruct((rows, cells), jnp.float32)] * groups,
        compiler_params=params(),
        cost_estimate=pl.CostEstimate(
            flops=6 * cells * length * rows * groups, bytes_accessed=8 * cells * length, transcendentals=0
        ),
        name="z_forward",
    )(me, field, table, *after)


def y_rows(table_ref, own, groups, plane_y):
    picked = [
        table_ref[pl.ds(pl.multiple_of((own ^ d) * plane_y, 8), plane_y), :] for d in range(groups)
    ]
    return halves(jnp.concatenate(picked, axis=0))


def y_forward(parts, table, lines, me, chunk, rows, plane_x, plane_y, after):
    groups = len(parts)
    length = table.shape[0]
    per = length // groups

    def kernel(me_ref, *refs):
        part_refs = refs[:groups]
        table_ref, lines_ref = refs[groups : groups + 2]
        spec_ref, ends_ref, gathered = refs[-3:]
        own = me_ref[0]
        right = y_rows(table_ref, own, groups, plane_y)
        for x in range(plane_x):
            gathered[x * rows : (x + 1) * rows, :] = jnp.concatenate(
                [ref[:, x * plane_y : (x + 1) * plane_y] for ref in part_refs], axis=1
            )
        result = three_dots(halves(gathered[...]), right, ((1,), (0,)))
        gathered[...] = result
        first = pl.multiple_of(own * per + chunk * rows, 8)
        ratio = lines_ref[0, pl.ds(first, rows), :]
        mask = lines_ref[2, pl.ds(first, rows), :]
        for g in range(0, rows, 8):
            step = ratio[g : g + 8]
            keep = mask[g : g + 8]
            zero = jnp.zeros_like(step)
            one, two = zero, zero
            for x in range(plane_x):
                value = gathered[x * rows + g : x * rows + g + 8, :]
                one = value + step * one
                two = one + step * two
                spec_ref[x, g : g + 8, :] = value * keep
            ends_ref[0, g : g + 8, :] = one
            ends_ref[1, g : g + 8, :] = two
            one, two = zero, zero
            for x in reversed(range(plane_x)):
                value = gathered[x * rows + g : x * rows + g + 8, :]
                one = value + step * one
                two = one + step * two
            ends_ref[2, g : g + 8, :] = one
            ends_ref[3, g : g + 8, :] = two

    return pl.pallas_call(
        kernel,
        in_specs=[whole(pltpu.SMEM)] + [whole()] * (groups + 2) + anywhere(len(after)),
        out_specs=[whole(), whole()],
        out_shape=[
            jax.ShapeDtypeStruct((plane_x, rows, length), jnp.float32),
            jax.ShapeDtypeStruct((4, rows, length), jnp.float32),
        ],
        scratch_shapes=[pltpu.VMEM((plane_x * rows, length), jnp.float32)],
        compiler_params=params(),
        cost_estimate=pl.CostEstimate(
            flops=6 * plane_x * rows * length * length,
            bytes_accessed=8 * plane_x * rows * length,
            transcendentals=0,
        ),
        name="y_forward",
    )(me, *parts, table, lines, *after)


def leap_power(leap, exponent, top):
    result, factor, bit = None, leap, 1
    while bit < top:
        term = jnp.where((exponent & bit) != 0, factor, jnp.ones_like(factor))
        result = term if result is None else result * term
        factor = factor * factor
        bit *= 2
    return result


def join_ends(ends, other, lines, me, level, plane_x):
    rows, length = ends.shape[1:]

    def kernel(me_ref, ends_ref, other_ref, lines_ref, out_ref):
        first = pl.multiple_of(me_ref[2], 8)
        right_half = ((me_ref[1] >> level) & 1) == 1
        leap = lines_ref[1, pl.ds(first, rows), :]
        for _ in range(level):
            leap = leap * leap
        span = float(plane_x * 2**level)
        for side in (0, 1):
            mine = [ends_ref[2 * side + k] for k in range(2)]
            theirs = [other_ref[2 * side + k] for k in range(2)]
            nearest = right_half if side == 0 else jnp.logical_not(right_half)
            near = [jnp.where(nearest, mine[k], theirs[k]) for k in range(2)]
            away = [jnp.where(nearest, theirs[k], mine[k]) for k in range(2)]
            out_ref[2 * side] = near[0] + leap * away[0]
            out_ref[2 * side + 1] = near[1] + leap * (away[1] + span * away[0])

    return pl.pallas_call(
        kernel,
        in_specs=[whole(pltpu.SMEM)] + [whole()] * 3,
        out_specs=whole(),
        out_shape=jax.ShapeDtypeStruct(ends.shape, jnp.float32),
        compiler_params=params(),
        cost_estimate=pl.CostEstimate(
            flops=8 * rows * length, bytes_accessed=48 * rows * length, transcendentals=0
        ),
        name="join_ends",
    )(me, ends, other, lines)


def y_backward(spec, ends, others, table, lines, me, groups, plane_y, after):
    plane_x, rows, length = spec.shape
    levels = len(others)
    blocks = 2**levels

    def kernel(me_ref, spec_ref, ends_ref, *refs):
        other_refs = refs[:levels]
        table_ref, lines_ref = refs[levels : levels + 2]
        outs, work = refs[-1 - groups : -1], refs[-1]
        right = y_rows(table_ref, me_ref[0], groups, plane_y)
        place = me_ref[1]
        first = pl.multiple_of(me_ref[2], 8)
        gaps = ([], [])
        for level in range(levels):
            size = 2**level
            inside = place & (size - 1)
            on_right = ((place >> level) & 1) == 1
            wrap = blocks - 2 * size
            gaps[0].append(inside + jnp.where(on_right, 0, wrap))
            gaps[1].append(size - 1 - inside + jnp.where(on_right, wrap, 0))
        for g in range(0, rows, 8):
            at = pl.ds(pl.multiple_of(first + g, 8), 8)
            step, leap = lines_ref[0, at, :], lines_ref[1, at, :]
            wrap_one, wrap_two = lines_ref[6, at, :], lines_ref[7, at, :]
            power = jnp.ones_like(leap)
            for _ in range(blocks - 1):
                power = power * leap
            carries = []
            for side in (0, 1):
                far_one = ends_ref[2 * side, g : g + 8, :]
                far_two = ends_ref[2 * side + 1, g : g + 8, :]
                one = power * far_one
                two = power * (far_two + float(plane_x * (blocks - 1)) * far_one)
                for level in range(levels):
                    gap = gaps[side][level]
                    factor = leap_power(leap, gap, blocks)
                    far_one = other_refs[level][2 * side, g : g + 8, :]
                    far_two = other_refs[level][2 * side + 1, g : g + 8, :]
                    one = one + factor * far_one
                    two = two + factor * (far_two + (plane_x * gap).astype(jnp.float32) * far_one)
                carries.append((one * wrap_one, two * wrap_one + wrap_two * one))
            weight_zero, weight_one, weight_two = lines_ref[3, at, :], lines_ref[4, at, :], lines_ref[5, at, :]
            one, two = carries[0]
            for x in range(plane_x):
                value = spec_ref[x, g : g + 8, :]
                one = value + step * one
                two = one + step * two
                work[x * rows + g : x * rows + g + 8, :] = (
                    weight_zero * value + weight_one * one + weight_two * two
                )
            one, two = carries[1]
            for x in reversed(range(plane_x)):
                value = spec_ref[x, g : g + 8, :]
                one = value + step * one
                two = one + step * two
                work[x * rows + g : x * rows + g + 8, :] += weight_one * one + weight_two * two
        work[...] = three_dots(halves(work[...]), right, ((1,), (1,)))
        pack = max(1, 128 // plane_y)
        for x in range(0, plane_x, pack):
            for d in range(groups):
                outs[d][:, x * plane_y : (x + pack) * plane_y] = jnp.concatenate(
                    [
                        work[(x + k) * rows : (x + k + 1) * rows, d * plane_y : (d + 1) * plane_y]
                        for k in range(pack)
                    ],
                    axis=1,
                )

    return pl.pallas_call(
        kernel,
        in_specs=[whole(pltpu.SMEM)] + [whole()] * (levels + 4) + anywhere(len(after)),
        out_specs=[whole()] * groups,
        out_shape=[jax.ShapeDtypeStruct((rows, plane_x * plane_y), jnp.float32)] * groups,
        scratch_shapes=[pltpu.VMEM((plane_x * rows, length), jnp.float32)],
        compiler_params=params(),
        cost_estimate=pl.CostEstimate(
            flops=6 * plane_x * rows * length * length,
            bytes_accessed=8 * plane_x * rows * length,
            transcendentals=0,
        ),
        name="y_backward",
    )(me, spec, ends, *others, table, lines, *after)


def segment_rows(vectors, offsets, cells, counts, pairs, me, plane_y, length, after):
    blocks, width = cells.shape

    def kernel(counts_ref, me_ref, vectors_ref, offsets_ref, cells_ref, pairs_ref, after_ref, out_ref, places_ref):
        cell = cells_ref[...]
        out_ref[0] = (cell // (length * plane_y)).astype(jnp.float32) + offsets_ref[0]
        out_ref[1] = (cell // length % plane_y).astype(jnp.float32) + offsets_ref[1]
        out_ref[2] = (cell % length).astype(jnp.float32) + offsets_ref[2]
        lane = lax.broadcasted_iota(jnp.int32, (1, width), 1)
        for b in range(blocks):
            live = lane < counts_ref[b]
            for k in range(3):
                out_ref[3 + k, b : b + 1, :] = jnp.where(live, vectors_ref[k, b : b + 1, :], 0.0)
        for k in range(3):
            out_ref[6 + k] = vectors_ref[3 + k]
        number = pairs_ref[...]
        column = number // blocks % 3
        even = jnp.full_like(number, me_ref[0]) & 1 == 0
        slot = jnp.where(column == 1, 0, jnp.where((column == 2) == even, 1, 2))
        places_ref[...] = (slot * 3 + number // (3 * blocks)) * blocks + number % blocks

    return pl.pallas_call(
        kernel,
        in_specs=[whole(pltpu.SMEM)] * 2 + [whole()] * 4 + [pl.BlockSpec(memory_space=pl.ANY)],
        out_specs=[whole()] * 2,
        out_shape=[
            jax.ShapeDtypeStruct((9, blocks, width), jnp.float32),
            jax.ShapeDtypeStruct(pairs.shape, jnp.int32),
        ],
        compiler_params=params(),
        name="segment_rows",
    )(counts, me, vectors, offsets, cells, pairs, after)


def z_backward(parts, table, cells, me, groups, chunks, rows, pull, source):
    cell_total = parts[0].shape[1]
    length = table.shape[0]
    per = length // groups
    seg_total = cells.shape[1]
    blocks, width = pull.shape[1:]
    tile = min(512, cell_total)
    steps = cell_total // tile

    def kernel(me_ref, *refs):
        part_refs, refs = refs[: groups * chunks], refs[groups * chunks :]
        table_ref, cells_ref, pull_ref, source_ref, stress_ref, force_ref, field, sems = refs
        own = me_ref[0]
        picked = [
            table_ref[pl.ds(pl.multiple_of((own ^ d) * per + c * rows, 8), rows), :]
            for c in range(chunks)
            for d in range(groups)
        ]
        right = halves(jnp.concatenate(picked, axis=0))
        left = halves(jnp.concatenate([ref[...] for ref in part_refs], axis=0))
        writes = []
        for i in range(steps):
            at = slice(i * tile, (i + 1) * tile)
            field[at, :] = three_dots([half[:, at] for half in left], right, ((0,), (0,)))
            writes.append(pltpu.make_async_copy(field.at[at], stress_ref.at[at], sems.at[i]))
            writes[-1].start()
        both = jnp.concatenate(left, axis=0)
        place = cells_ref[...] // length
        depth = cells_ref[...] % length
        lane_tile = min(512, seg_total)
        taus = []
        for k in range(0, seg_total, lane_tile):
            at = slice(k, k + lane_tile)
            hot = jnp.where(
                lax.broadcasted_iota(jnp.int32, (cell_total, lane_tile), 0) == place[:, at], 1.0, 0.0
            ).astype(jnp.bfloat16)
            found = jnp.dot(both, hot, preferred_element_type=jnp.float32)
            hot_z = jnp.where(
                lax.broadcasted_iota(jnp.int32, (length, lane_tile), 0) == depth[:, at], 1.0, 0.0
            ).astype(jnp.bfloat16)
            factor = jnp.dot(jnp.concatenate(right, axis=0), hot_z, preferred_element_type=jnp.float32)
            tau = jnp.sum(
                (found[:length] + found[length:]) * (factor[:length] + factor[length:]), axis=0, keepdims=True
            )
            taus += [tau[:, j : j + width] for j in range(0, lane_tile, width)]
        tau = jnp.concatenate(taus, axis=0)
        b0, b1, b2, t0, t1, t2 = (source_ref[3 + k] for k in range(6))
        force_ref[0] = pull_ref[0] + tau * (b1 * t2 - b2 * t1)
        force_ref[1] = pull_ref[1] + tau * (b2 * t0 - b0 * t2)
        force_ref[2] = pull_ref[2] + tau * (b0 * t1 - b1 * t0)
        for write in writes:
            write.wait()

    return pl.pallas_call(
        kernel,
        in_specs=[whole(pltpu.SMEM)] + [whole()] * (groups * chunks + 4),
        out_specs=anywhere(1) + [whole()],
        out_shape=[
            jax.ShapeDtypeStruct((cell_total, length), jnp.float32),
            jax.ShapeDtypeStruct((3, blocks, width), jnp.float32),
        ],
        scratch_shapes=[pltpu.VMEM((cell_total, length), jnp.float32), pltpu.SemaphoreType.DMA((steps,))],
        compiler_params=params(),
        cost_estimate=pl.CostEstimate(
            flops=6 * cell_total * length * length, bytes_accessed=8 * cell_total * length, transcendentals=0
        ),
        name="z_backward",
    )(me, *parts, table, cells, pull, source)


def join_rows(low, own, high, after):
    rows = own.shape[0]

    def kernel(low_ref, own_ref, high_ref, after_ref, out_ref):
        out_ref[0:rows] = low_ref[...]
        out_ref[rows : 2 * rows] = own_ref[...]
        out_ref[2 * rows :] = high_ref[...]

    return pl.pallas_call(
        kernel,
        in_specs=[whole()] * 3 + anywhere(1),
        out_specs=whole(),
        out_shape=jax.ShapeDtypeStruct((3 * rows,) + own.shape[1:], jnp.float32),
        compiler_params=params(),
        name="join_rows",
    )(low, own, high, after)


def spread_rows(source, after):
    rows, blocks, width = source.shape

    def kernel(source_ref, *refs):
        near = refs[-1]
        spread_row = lax.broadcasted_iota(jnp.int32, (3 * rows, rows * width), 0) % rows
        spread_col = lax.broadcasted_iota(jnp.int32, (3 * rows, rows * width), 1) // width
        spread = (spread_row == spread_col).astype(jnp.bfloat16)
        for b in range(blocks):
            own = jnp.concatenate([source_ref[k, b : b + 1, :] for k in range(rows)], axis=0)
            high = own.astype(jnp.bfloat16).astype(jnp.float32)
            rest = own - high
            middle = rest.astype(jnp.bfloat16).astype(jnp.float32)
            split = jnp.concatenate([high, middle, rest - middle], axis=0).astype(jnp.bfloat16)
            near[b * width : (b + 1) * width, :] = lax.dot_general(
                split, spread, (((0,), (0,)), ((), ())), preferred_element_type=jnp.float32
            )

    return pl.pallas_call(
        kernel,
        in_specs=[whole()] + anywhere(len(after)),
        out_specs=whole(),
        out_shape=jax.ShapeDtypeStruct((blocks * width, rows * width), jnp.float32),
        compiler_params=params(),
        name="spread_rows",
    )(source, *after)


def gather_rows(trios, me, plane_x, plane_y):
    blocks, width = trios[0].shape[1:]
    rows = trios[0].shape[0] // 3
    stride = rows * blocks
    padded = (9 * blocks + 127) // 128 * 128

    def kernel(me_ref, *refs):
        trio_refs = refs[:3]
        far, marks, flags = refs[3:]
        toward = jnp.where(me_ref[0] & 1 == 1, -float(plane_y), float(plane_y))
        flags[...] = jnp.zeros_like(flags)
        for slot in range(3):
            for p in range(3):
                base = slot * 3 + p
                trio = trio_refs[slot]
                for k in range(rows):
                    value = trio[p * rows + k]
                    if k == 0 and p != 1:
                        value = value + float((p - 1) * plane_x)
                    if k == 1 and slot > 0:
                        value = value + (toward if slot == 1 else -toward)
                    at = base * stride + k * blocks
                    far[at : at + blocks, :] = value
                size = jnp.maximum(
                    jnp.maximum(jnp.abs(trio[p * rows + 3]), jnp.abs(trio[p * rows + 4])),
                    jnp.abs(trio[p * rows + 5]),
                )
                flags[base * blocks : (base + 1) * blocks, :] = (size > 0.0).astype(jnp.float32)
        marks[...] = lax.dot_general(
            jnp.ones((8, width), jnp.bfloat16),
            flags[...].astype(jnp.bfloat16),
            (((1,), (1,)), ((), ())),
            preferred_element_type=jnp.float32,
        ).astype(jnp.int32)

    return pl.pallas_call(
        kernel,
        in_specs=[whole(pltpu.SMEM)] + [whole()] * 3,
        out_specs=[whole()] * 2,
        out_shape=[
            jax.ShapeDtypeStruct((9 * stride, width), jnp.float32),
            jax.ShapeDtypeStruct((8, padded), jnp.int32),
        ],
        scratch_shapes=[pltpu.VMEM((padded, width), jnp.float32)],
        compiler_params=params(),
        name="gather_rows",
    )(me, *trios)


def pair_pull(near, far, marks, pairs, after):
    blocks, partners = pairs.shape
    width = near.shape[0] // blocks
    rows = near.shape[1] // width
    stride = rows * blocks

    def kernel(pairs_ref, marks_ref, near, far, *refs):
        out_ref, total = refs[-2:]
        total[...] = jnp.zeros_like(total)

        def one_block(b, carry):
            own_at = pl.multiple_of(b * width, width)

            def one_partner(p, carry):
                number = pairs_ref[b, p]

                @pl.when(marks_ref[0, number] > 0)
                def _():
                    first = number // blocks * stride + number % blocks
                    other = [
                        jnp.broadcast_to(far[pl.ds(first + k * blocks, 1), :], (8, width)) for k in range(rows)
                    ]
                    for t in range(0, width, 8):
                        at = pl.ds(pl.multiple_of(own_at + t, 8), 8)
                        mine = [near[at, k * width : (k + 1) * width] for k in range(rows)]
                        dx, dy, dz = (mine[k] - other[k] for k in range(3))
                        inverse = lax.rsqrt(dx * dx + dy * dy + dz * dz + core_sq)
                        squared = inverse * inverse
                        burg_dot = mine[3] * other[3] + mine[4] * other[4] + mine[5] * other[5]
                        line_dot = mine[6] * other[6] + mine[7] * other[7] + mine[8] * other[8]
                        burg_own = mine[3] * dx + mine[4] * dy + mine[5] * dz
                        burg_far = other[3] * dx + other[4] * dy + other[5] * dz
                        weight = (line_dot * (squared * inverse)) * (
                            burg_dot - (3.0 * squared) * (burg_own * burg_far)
                        )
                        total[0, at, :] += weight * dx
                        total[1, at, :] += weight * dy
                        total[2, at, :] += weight * dz

                return carry

            return lax.fori_loop(0, partners, one_partner, carry)

        lax.fori_loop(0, blocks, one_block, 0)
        ones = jnp.ones((8, width), jnp.bfloat16)
        dims = (((1,), (1,)), ((), ()))
        for k in range(3):
            high, low = halves(total[k])
            summed = lax.dot_general(ones, high, dims, preferred_element_type=jnp.float32) + lax.dot_general(
                ones, low, dims, preferred_element_type=jnp.float32
            )
            for b in range(blocks):
                out_ref[k, b : b + 1, :] = pair_scale * summed[0:1, b * width : (b + 1) * width]

    return pl.pallas_call(
        kernel,
        in_specs=[whole(pltpu.SMEM)] * 2 + [whole()] * 2 + anywhere(len(after)),
        out_specs=whole(),
        out_shape=jax.ShapeDtypeStruct((3, blocks, width), jnp.float32),
        scratch_shapes=[pltpu.VMEM((3, blocks * width, width), jnp.float32)],
        compiler_params=params(),
        cost_estimate=pl.CostEstimate(
            flops=50 * blocks * partners * width * width,
            bytes_accessed=36 * stride * width,
            transcendentals=blocks * partners * width * width,
        ),
        name="pair_pull",
    )(pairs, marks, near, far, *after)


def per_device(eigen, seg_vec, seg_off, seg_cell, blk_count, pair_list):
    plane_x, plane_y, length = eigen.shape
    groups_x = lax.axis_size("gx")
    groups_y = lax.axis_size("gy")
    per = length // groups_y
    chunks = CHUNKS if per // CHUNKS >= 8 else 1
    rows = per // chunks
    place_x = lax.axis_index("gx").astype(jnp.int32)
    place_y = lax.axis_index("gy").astype(jnp.int32)
    mes = [jnp.stack([place_y, place_x, place_y * per + c * rows]) for c in range(chunks)]
    me = mes[0]
    table = jnp.asarray(hartley_table(length))
    lines = jnp.asarray(line_tables(length, plane_x))

    def swap(parts):
        return [parts[0]] + [
            lax.ppermute(parts[d], "gy", [(i, i ^ d) for i in range(groups_y)])
            for d in range(1, groups_y)
        ]

    field = eigen.reshape(plane_x * plane_y, length)
    sent = []
    for c in range(chunks):
        sent.append(z_forward(field, table, me, groups_y, c, rows, sent[-1][:1] if sent else []))
    arrived = [swap(parts) for parts in sent]

    seg_total = seg_cell.shape[2]
    block_total = blk_count.shape[2]
    width = seg_total // block_total
    cells = seg_cell.reshape(block_total, width)
    source, pairs = segment_rows(
        seg_vec.reshape(6, block_total, width),
        seg_off.reshape(3, block_total, width),
        cells,
        blk_count.reshape(block_total),
        pair_list.reshape(block_total, pair_list.shape[3]),
        me,
        plane_y,
        length,
        sent[-1][0],
    )
    low = lax.ppermute(source, "gx", [(i, (i + 1) % groups_x) for i in range(groups_x)])
    high = lax.ppermute(source, "gx", [((i + 1) % groups_x, i) for i in range(groups_x)])

    near = spread_rows(source, [])

    forward = []
    for c in range(chunks):
        after = [low, high, near] if c == 0 else [forward[-1][1]]
        forward.append(y_forward(arrived[c], table, lines, me, c, rows, plane_x, plane_y, after))
    trio = join_rows(low, source, high, forward[-1][1])
    other = [(i, (i + 1 if i % 2 else i - 1) % groups_y) for i in range(groups_y)]
    trios = [
        trio,
        lax.ppermute(trio, "gy", [(i, i ^ 1) for i in range(groups_y)]),
        lax.ppermute(trio, "gy", other),
    ]

    far, marks = gather_rows(trios, me, plane_x, plane_y)

    returned = []
    for c in range(chunks):
        spec, ends = forward[c]
        others, joined, level = [], ends, 0
        while 2**level < groups_x:
            others.append(lax.ppermute(joined, "gx", [(i, i ^ 2**level) for i in range(groups_x)]))
            if 2 ** (level + 1) < groups_x:
                joined = join_ends(joined, others[-1], lines, mes[c], level, plane_x)
            level += 1
        after = [returned[-1][0], far] if c else []
        returned.append(y_backward(spec, ends, others, table, lines, mes[c], groups_y, plane_y, after))
    landed = [swap(parts) for parts in returned]

    pull = pair_pull(near, far, marks, pairs, [returned[-1][0]])
    flat = [part for parts in landed for part in parts]
    stress, force = z_backward(
        flat, table, seg_cell.reshape(1, seg_total), me, groups_y, chunks, rows, pull, source
    )
    return stress.reshape(eigen.shape), force.reshape(3, 1, 1, seg_total)


def solution(mesh):
    return jax.shard_map(
        per_device,
        mesh=mesh,
        in_specs=(
            P("gx", "gy", None),
            P(None, "gx", "gy", None),
            P(None, "gx", "gy", None),
            P("gx", "gy", None),
            P("gx", "gy", None),
            P("gx", "gy", None, None),
        ),
        out_specs=(P("gx", "gy", None), P(None, "gx", "gy", None)),
        check_vma=False,
    )
```

```python
import math

import jax
import jax.numpy as jnp
import numpy as np
from jax import lax
from jax.experimental import pallas as pl
from jax.experimental.pallas import tpu as pltpu
from jax.sharding import PartitionSpec as P

nu_copper = 0.34
core_sq = 4.0
pair_scale = 4.0
CHUNKS = (32, 32)
SHARES = (5, 11)
ORDER = ()
VMEM_LIMIT = 24 * 1024 * 1024
COSTS = {'join_ends': (0.0, 3.0, 0.0, 0.0), 'pair_pull': (1.5, 0.0)}


def counted(cost):
    return pl.CostEstimate(flops=int(cost * 1e9), bytes_accessed=0, transcendentals=0)


def hartley_table(length):
    phase = np.outer(np.arange(length), np.arange(length)) % length
    angle = phase * (2.0 * math.pi / length)
    return ((np.cos(angle) + np.sin(angle)) / math.sqrt(length)).astype(np.float32)


def line_tables(length, plane_x):
    freq = np.arange(length, dtype=np.float64)
    wave = (2.0 * np.sin(math.pi * freq / length)) ** 2
    wave_z = wave[:, None]
    wave_y = wave[None, :]
    total = wave_y + wave_z
    zero = total == 0.0
    safe = np.where(zero, 1.0, total)
    ratio = 1.0 / (1.0 + safe / 2.0 + np.sqrt(safe + safe * safe / 4.0))
    ratio = ratio.astype(np.float32).astype(np.float64)
    elastic = 2.0 / (1.0 - nu_copper)
    gap = 1.0 - ratio * ratio
    green = ratio / gap
    first = -2.0 * (wave_y + elastic * wave_z) * green
    second = 2.0 * elastic * wave_z * safe * green * green
    weight_two = second
    weight_one = first + second * 2.0 * ratio * ratio / gap
    weight_zero = -first - second * (1.0 + ratio * ratio) / gap
    lap = ratio**length
    wrap_one = 1.0 / (1.0 - lap)
    wrap_two = length * lap / (1.0 - lap) ** 2
    leap = ratio**plane_x
    mask = np.where(zero, 0.0, 1.0)
    ratio = np.where(zero, 1.0, ratio)
    leap = np.where(zero, 1.0, leap)
    weight_zero = np.where(zero, 0.0, weight_zero)
    weight_one = np.where(zero, -1.0 / length, weight_one)
    weight_two = np.where(zero, 0.0, weight_two)
    wrap_one = np.where(zero, 1.0, wrap_one)
    wrap_two = np.where(zero, 0.0, wrap_two)
    tables = [ratio, leap, mask, weight_zero, weight_one, weight_two, wrap_one, wrap_two]
    return np.stack([t.astype(np.float32) for t in tables])


def halves(value):
    high = value.astype(jnp.bfloat16)
    low = (value - high.astype(jnp.float32)).astype(jnp.bfloat16)
    return high, low


def three_dots(left, right, dims):
    def one(a, b):
        return lax.dot_general(a, b, (dims, ((), ())), preferred_element_type=jnp.float32)

    return one(left[0], right[0]) + one(left[0], right[1]) + one(left[1], right[0])


def whole(memory=pltpu.VMEM):
    return pl.BlockSpec(memory_space=memory)


def anywhere(count):
    return [pl.BlockSpec(memory_space=pl.ANY)] * count


def params():
    return pltpu.CompilerParams(vmem_limit_bytes=VMEM_LIMIT)


def z_forward(field, table, me, groups, offset, rows, after, cost):
    cells, length = field.shape
    per = length // groups
    depth = groups * rows

    def kernel(me_ref, field_ref, table_ref, *refs):
        outs = refs[-groups:]
        own = me_ref[0]
        picked = [
            table_ref[pl.ds(pl.multiple_of((own ^ d) * per + offset, 8), rows), :] for d in range(groups)
        ]
        left = halves(jnp.concatenate(picked, axis=0))
        right = halves(field_ref[...])
        dims = (((1,), (1,)), ((), ()))
        both = lax.dot_general(
            jnp.concatenate(left, axis=0), right[0], dims, preferred_element_type=jnp.float32
        )
        result = both[:depth] + both[depth:]
        result = result + lax.dot_general(left[0], right[1], dims, preferred_element_type=jnp.float32)
        for d in range(groups):
            outs[d][...] = result[d * rows : (d + 1) * rows]

    return pl.pallas_call(
        kernel,
        in_specs=[whole(pltpu.SMEM)] + [whole()] * 2 + anywhere(len(after)),
        out_specs=[whole()] * groups,
        out_shape=[jax.ShapeDtypeStruct((rows, cells), jnp.float32)] * groups,
        compiler_params=params(),
        cost_estimate=counted(cost),
        name="z_forward",
    )(me, field, table, *after)


def y_rows(table_ref, own, groups, plane_y):
    picked = [
        table_ref[pl.ds(pl.multiple_of((own ^ d) * plane_y, 8), plane_y), :] for d in range(groups)
    ]
    return halves(jnp.concatenate(picked, axis=0))


def y_forward(parts, table, lines, me, offset, rows, plane_x, plane_y, after, cost):
    groups = len(parts)
    length = table.shape[0]
    per = length // groups

    def kernel(me_ref, *refs):
        part_refs = refs[:groups]
        table_ref, all_lines = refs[groups : groups + 2]
        spec_ref, ends_ref, lines_ref, gathered, lines_sem = refs[-5:]
        own = me_ref[0]
        first = pl.multiple_of(own * per + offset, 8)
        fetch = pltpu.make_async_copy(all_lines.at[:, pl.ds(first, rows)], lines_ref, lines_sem)
        fetch.start()
        right = y_rows(table_ref, own, groups, plane_y)
        for x in range(plane_x):
            gathered[x * rows : (x + 1) * rows, :] = jnp.concatenate(
                [ref[:, x * plane_y : (x + 1) * plane_y] for ref in part_refs], axis=1
            )
        result = three_dots(halves(gathered[...]), right, ((1,), (0,)))
        gathered[...] = result
        fetch.wait()
        ratio = lines_ref[0]
        mask = lines_ref[2]
        for g in range(0, rows, 8):
            step = ratio[g : g + 8]
            keep = mask[g : g + 8]
            zero = jnp.zeros_like(step)
            one, two = zero, zero
            for x in range(plane_x):
                value = gathered[x * rows + g : x * rows + g + 8, :]
                one = value + step * one
                two = one + step * two
                spec_ref[x, g : g + 8, :] = value * keep
            ends_ref[0, g : g + 8, :] = one
            ends_ref[1, g : g + 8, :] = two
            one, two = zero, zero
            for x in reversed(range(plane_x)):
                value = gathered[x * rows + g : x * rows + g + 8, :]
                one = value + step * one
                two = one + step * two
            ends_ref[2, g : g + 8, :] = one
            ends_ref[3, g : g + 8, :] = two

    return pl.pallas_call(
        kernel,
        in_specs=[whole(pltpu.SMEM)] + [whole()] * (groups + 1) + anywhere(1 + len(after)),
        out_specs=[whole()] * 3,
        out_shape=[
            jax.ShapeDtypeStruct((plane_x, rows, length), jnp.float32),
            jax.ShapeDtypeStruct((4, rows, length), jnp.float32),
            jax.ShapeDtypeStruct((lines.shape[0], rows, length), jnp.float32),
        ],
        scratch_shapes=[pltpu.VMEM((plane_x * rows, length), jnp.float32), pltpu.SemaphoreType.DMA],
        compiler_params=params(),
        cost_estimate=counted(cost),
        name="y_forward",
    )(me, *parts, table, lines, *after)


def leap_power(leap, exponent, top):
    result, factor, bit = None, leap, 1
    while bit < top:
        term = jnp.where((exponent & bit) != 0, factor, jnp.ones_like(factor))
        result = term if result is None else result * term
        factor = factor * factor
        bit *= 2
    return result


def join_ends(ends, other, lines, me, level, plane_x, after, cost):
    rows, length = ends.shape[1:]

    def kernel(me_ref, ends_ref, other_ref, lines_ref, *refs):
        out_ref = refs[-1]
        right_half = ((me_ref[1] >> level) & 1) == 1
        leap = lines_ref[1]
        for _ in range(level):
            leap = leap * leap
        span = float(plane_x * 2**level)
        for side in (0, 1):
            mine = [ends_ref[2 * side + k] for k in range(2)]
            theirs = [other_ref[2 * side + k] for k in range(2)]
            nearest = right_half if side == 0 else jnp.logical_not(right_half)
            near = [jnp.where(nearest, mine[k], theirs[k]) for k in range(2)]
            away = [jnp.where(nearest, theirs[k], mine[k]) for k in range(2)]
            out_ref[2 * side] = near[0] + leap * away[0]
            out_ref[2 * side + 1] = near[1] + leap * (away[1] + span * away[0])

    return pl.pallas_call(
        kernel,
        in_specs=[whole(pltpu.SMEM)] + [whole()] * 3 + anywhere(len(after)),
        out_specs=whole(),
        out_shape=jax.ShapeDtypeStruct(ends.shape, jnp.float32),
        compiler_params=params(),
        cost_estimate=counted(cost),
        name="join_ends",
    )(me, ends, other, lines, *after)


def y_backward(spec, ends, others, table, lines, me, groups, plane_y, after, cost):
    plane_x, rows, length = spec.shape
    levels = len(others)
    blocks = 2**levels

    def kernel(me_ref, spec_ref, ends_ref, *refs):
        other_refs = refs[:levels]
        table_ref, lines_ref = refs[levels : levels + 2]
        outs, work = refs[-1 - groups : -1], refs[-1]
        right = y_rows(table_ref, me_ref[0], groups, plane_y)
        place = me_ref[1]
        gaps = ([], [])
        for level in range(levels):
            size = 2**level
            inside = place & (size - 1)
            on_right = ((place >> level) & 1) == 1
            wrap = blocks - 2 * size
            gaps[0].append(inside + jnp.where(on_right, 0, wrap))
            gaps[1].append(size - 1 - inside + jnp.where(on_right, wrap, 0))
        for g in range(0, rows, 8):
            at = slice(g, g + 8)
            step, leap = lines_ref[0, at, :], lines_ref[1, at, :]
            wrap_one, wrap_two = lines_ref[6, at, :], lines_ref[7, at, :]
            power = jnp.ones_like(leap)
            for _ in range(blocks - 1):
                power = power * leap
            carries = []
            for side in (0, 1):
                far_one = ends_ref[2 * side, g : g + 8, :]
                far_two = ends_ref[2 * side + 1, g : g + 8, :]
                one = power * far_one
                two = power * (far_two + float(plane_x * (blocks - 1)) * far_one)
                for level in range(levels):
                    gap = gaps[side][level]
                    factor = leap_power(leap, gap, blocks)
                    far_one = other_refs[level][2 * side, g : g + 8, :]
                    far_two = other_refs[level][2 * side + 1, g : g + 8, :]
                    one = one + factor * far_one
                    two = two + factor * (far_two + (plane_x * gap).astype(jnp.float32) * far_one)
                carries.append((one * wrap_one, two * wrap_one + wrap_two * one))
            weight_zero, weight_one, weight_two = lines_ref[3, at, :], lines_ref[4, at, :], lines_ref[5, at, :]
            one, two = carries[0]
            for x in range(plane_x):
                value = spec_ref[x, g : g + 8, :]
                one = value + step * one
                two = one + step * two
                work[x * rows + g : x * rows + g + 8, :] = (
                    weight_zero * value + weight_one * one + weight_two * two
                )
            one, two = carries[1]
            for x in reversed(range(plane_x)):
                value = spec_ref[x, g : g + 8, :]
                one = value + step * one
                two = one + step * two
                work[x * rows + g : x * rows + g + 8, :] += weight_one * one + weight_two * two
        work[...] = three_dots(halves(work[...]), right, ((1,), (1,)))
        pack = max(1, 128 // plane_y)
        for x in range(0, plane_x, pack):
            for d in range(groups):
                outs[d][:, x * plane_y : (x + pack) * plane_y] = jnp.concatenate(
                    [
                        work[(x + k) * rows : (x + k + 1) * rows, d * plane_y : (d + 1) * plane_y]
                        for k in range(pack)
                    ],
                    axis=1,
                )

    return pl.pallas_call(
        kernel,
        in_specs=[whole(pltpu.SMEM)] + [whole()] * (levels + 4) + anywhere(len(after)),
        out_specs=[whole()] * groups,
        out_shape=[jax.ShapeDtypeStruct((rows, plane_x * plane_y), jnp.float32)] * groups,
        scratch_shapes=[pltpu.VMEM((plane_x * rows, length), jnp.float32)],
        compiler_params=params(),
        cost_estimate=counted(cost),
        name="y_backward",
    )(me, spec, ends, *others, table, lines, *after)


def segment_rows(vectors, offsets, cells, counts, pairs, me, plane_y, length, after, cost):
    blocks, width = cells.shape

    def kernel(counts_ref, me_ref, vectors_ref, offsets_ref, cells_ref, pairs_ref, after_ref, out_ref, places_ref):
        cell = cells_ref[...]
        out_ref[0] = (cell // (length * plane_y)).astype(jnp.float32) + offsets_ref[0]
        out_ref[1] = (cell // length % plane_y).astype(jnp.float32) + offsets_ref[1]
        out_ref[2] = (cell % length).astype(jnp.float32) + offsets_ref[2]
        lane = lax.broadcasted_iota(jnp.int32, (1, width), 1)
        for b in range(blocks):
            live = lane < counts_ref[b]
            for k in range(3):
                out_ref[3 + k, b : b + 1, :] = jnp.where(live, vectors_ref[k, b : b + 1, :], 0.0)
        for k in range(3):
            out_ref[6 + k] = vectors_ref[3 + k]
        number = pairs_ref[...]
        column = number // blocks % 3
        even = jnp.full_like(number, me_ref[0]) & 1 == 0
        slot = jnp.where(column == 1, 0, jnp.where((column == 2) == even, 1, 2))
        places_ref[...] = (slot * 3 + number // (3 * blocks)) * blocks + number % blocks

    return pl.pallas_call(
        kernel,
        in_specs=[whole(pltpu.SMEM)] * 2 + [whole()] * 4 + [pl.BlockSpec(memory_space=pl.ANY)],
        out_specs=[whole()] * 2,
        out_shape=[
            jax.ShapeDtypeStruct((9, blocks, width), jnp.float32),
            jax.ShapeDtypeStruct(pairs.shape, jnp.int32),
        ],
        compiler_params=params(),
        cost_estimate=counted(cost),
        name="segment_rows",
    )(counts, me, vectors, offsets, cells, pairs, after)


def z_backward(parts, table, cells, me, groups, offset, rows, before, pull, source, after, cost):
    cell_total = parts[0].shape[1]
    length = table.shape[0]
    per = length // groups
    depth = groups * rows
    seg_total = cells.shape[1]
    blocks, width = source.shape[1:]
    tile = min(512, cell_total)
    steps = cell_total // tile
    adds = before is not None
    last = pull is not None

    def kernel(me_ref, *refs):
        part_refs, refs = refs[:groups], refs[groups:]
        table_ref, cells_ref, source_ref, refs = refs[0], refs[1], refs[2], refs[3:]
        if adds:
            old_ref, old_tau_ref, refs = refs[0], refs[1], refs[2:]
        if last:
            pull_ref, refs = refs[0], refs[1:]
            stress_ref, out_ref, field, sems = refs[-4:]
        else:
            field, out_ref = refs[-2:]
        own = me_ref[0]
        picked = [
            table_ref[pl.ds(pl.multiple_of((own ^ d) * per + offset, 8), rows), :]
            for d in range(groups)
        ]
        right = halves(jnp.concatenate(picked, axis=0))
        left = halves(jnp.concatenate([ref[...] for ref in part_refs], axis=0))
        both = jnp.concatenate(left, axis=0)
        twice = jnp.concatenate([right[0], right[0]], axis=0)
        writes = []
        for i in range(steps):
            at = slice(i * tile, (i + 1) * tile)
            share = lax.dot_general(
                both[:, at], twice, (((0,), (0,)), ((), ())), preferred_element_type=jnp.float32
            ) + lax.dot_general(
                left[0][:, at], right[1], (((0,), (0,)), ((), ())), preferred_element_type=jnp.float32
            )
            field[at, :] = share + old_ref[at, :] if adds else share
            if last:
                writes.append(
                    pltpu.make_async_copy(
                        field.at[pl.ds(i * tile, tile)], stress_ref.at[pl.ds(i * tile, tile)], sems.at[i]
                    )
                )
                writes[-1].start()
        place = cells_ref[...] // length
        level = cells_ref[...] % length
        lane_tile = min(512, seg_total)
        taus = []
        for k in range(0, seg_total, lane_tile):
            at = slice(k, k + lane_tile)
            hot = jnp.where(
                lax.broadcasted_iota(jnp.int32, (cell_total, lane_tile), 0) == place[:, at], 1.0, 0.0
            ).astype(jnp.bfloat16)
            found = jnp.dot(both, hot, preferred_element_type=jnp.float32)
            hot_z = jnp.where(
                lax.broadcasted_iota(jnp.int32, (length, lane_tile), 0) == level[:, at], 1.0, 0.0
            ).astype(jnp.bfloat16)
            factor = jnp.dot(jnp.concatenate(right, axis=0), hot_z, preferred_element_type=jnp.float32)
            tau = jnp.sum(
                (found[:depth] + found[depth:]) * (factor[:depth] + factor[depth:]), axis=0, keepdims=True
            )
            taus += [tau[:, j : j + width] for j in range(0, lane_tile, width)]
        tau = jnp.concatenate(taus, axis=0)
        if adds:
            tau = tau + old_tau_ref[...]
        if last:
            b0, b1, b2, t0, t1, t2 = (source_ref[3 + k] for k in range(6))
            out_ref[0] = pull_ref[0] + tau * (b1 * t2 - b2 * t1)
            out_ref[1] = pull_ref[1] + tau * (b2 * t0 - b0 * t2)
            out_ref[2] = pull_ref[2] + tau * (b0 * t1 - b1 * t0)
        else:
            out_ref[...] = tau
        for write in writes:
            write.wait()

    operands = [me, *parts, table, cells, source]
    if adds:
        operands += list(before)
    if last:
        operands.append(pull)
    scratch = [pltpu.VMEM((cell_total, length), jnp.float32), pltpu.SemaphoreType.DMA((steps,))]
    return pl.pallas_call(
        kernel,
        in_specs=[whole(pltpu.SMEM)] + [whole()] * (len(operands) - 1) + anywhere(len(after)),
        out_specs=(anywhere(1) if last else [whole()]) + [whole()],
        out_shape=[
            jax.ShapeDtypeStruct((cell_total, length), jnp.float32),
            jax.ShapeDtypeStruct((3, blocks, width) if last else (blocks, width), jnp.float32),
        ],
        scratch_shapes=scratch if last else [],
        compiler_params=params(),
        cost_estimate=counted(cost),
        name="z_backward",
    )(*operands, *after)


def join_rows(low, own, high, after, cost):
    rows = own.shape[0]

    def kernel(low_ref, own_ref, high_ref, after_ref, out_ref):
        out_ref[0:rows] = low_ref[...]
        out_ref[rows : 2 * rows] = own_ref[...]
        out_ref[2 * rows :] = high_ref[...]

    return pl.pallas_call(
        kernel,
        in_specs=[whole()] * 3 + anywhere(1),
        out_specs=whole(),
        out_shape=jax.ShapeDtypeStruct((3 * rows,) + own.shape[1:], jnp.float32),
        compiler_params=params(),
        cost_estimate=counted(cost),
        name="join_rows",
    )(low, own, high, after)


def spread_rows(source, after, cost):
    rows, blocks, width = source.shape

    def kernel(source_ref, *refs):
        near = refs[-1]
        spread_row = lax.broadcasted_iota(jnp.int32, (3 * rows, rows * width), 0) % rows
        spread_col = lax.broadcasted_iota(jnp.int32, (3 * rows, rows * width), 1) // width
        spread = (spread_row == spread_col).astype(jnp.bfloat16)
        for b in range(blocks):
            own = jnp.concatenate([source_ref[k, b : b + 1, :] for k in range(rows)], axis=0)
            high = own.astype(jnp.bfloat16).astype(jnp.float32)
            rest = own - high
            middle = rest.astype(jnp.bfloat16).astype(jnp.float32)
            split = jnp.concatenate([high, middle, rest - middle], axis=0).astype(jnp.bfloat16)
            near[b * width : (b + 1) * width, :] = lax.dot_general(
                split, spread, (((0,), (0,)), ((), ())), preferred_element_type=jnp.float32
            )

    return pl.pallas_call(
        kernel,
        in_specs=[whole()] + anywhere(len(after)),
        out_specs=whole(),
        out_shape=jax.ShapeDtypeStruct((blocks * width, rows * width), jnp.float32),
        compiler_params=params(),
        cost_estimate=counted(cost),
        name="spread_rows",
    )(source, *after)


def gather_rows(trios, me, plane_x, plane_y, cost):
    blocks, width = trios[0].shape[1:]
    rows = trios[0].shape[0] // 3
    stride = rows * blocks
    padded = (9 * blocks + 127) // 128 * 128

    def kernel(me_ref, *refs):
        trio_refs = refs[:3]
        far, marks, flags = refs[3:]
        toward = jnp.where(me_ref[0] & 1 == 1, -float(plane_y), float(plane_y))
        flags[...] = jnp.zeros_like(flags)
        for slot in range(3):
            for p in range(3):
                base = slot * 3 + p
                trio = trio_refs[slot]
                for k in range(rows):
                    value = trio[p * rows + k]
                    if k == 0 and p != 1:
                        value = value + float((p - 1) * plane_x)
                    if k == 1 and slot > 0:
                        value = value + (toward if slot == 1 else -toward)
                    at = base * stride + k * blocks
                    far[at : at + blocks, :] = value
                size = jnp.maximum(
                    jnp.maximum(jnp.abs(trio[p * rows + 3]), jnp.abs(trio[p * rows + 4])),
                    jnp.abs(trio[p * rows + 5]),
                )
                flags[base * blocks : (base + 1) * blocks, :] = (size > 0.0).astype(jnp.float32)
        marks[...] = lax.dot_general(
            jnp.ones((8, width), jnp.bfloat16),
            flags[...].astype(jnp.bfloat16),
            (((1,), (1,)), ((), ())),
            preferred_element_type=jnp.float32,
        ).astype(jnp.int32)

    return pl.pallas_call(
        kernel,
        in_specs=[whole(pltpu.SMEM)] + [whole()] * 3,
        out_specs=[whole()] * 2,
        out_shape=[
            jax.ShapeDtypeStruct((9 * stride, width), jnp.float32),
            jax.ShapeDtypeStruct((8, padded), jnp.int32),
        ],
        scratch_shapes=[pltpu.VMEM((padded, width), jnp.float32)],
        compiler_params=params(),
        cost_estimate=counted(cost),
        name="gather_rows",
    )(me, *trios)


def pair_pull(near, far, marks, pairs, first_block, count, after, cost):
    blocks, partners = pairs.shape
    width = near.shape[0] // blocks
    rows = near.shape[1] // width
    stride = rows * blocks

    def kernel(pairs_ref, marks_ref, near, far, *refs):
        out_ref, total = refs[-2:]
        total[...] = jnp.zeros_like(total)

        def one_block(index, carry):
            b = first_block + index
            own_at = pl.multiple_of(b * width, width)
            sum_at = pl.multiple_of(index * width, width)

            def one_partner(p, carry):
                number = pairs_ref[b, p]

                @pl.when(marks_ref[0, number] > 0)
                def _():
                    first = number // blocks * stride + number % blocks
                    other = [
                        jnp.broadcast_to(far[pl.ds(first + k * blocks, 1), :], (8, width)) for k in range(rows)
                    ]
                    for t in range(0, width, 8):
                        at = pl.ds(pl.multiple_of(own_at + t, 8), 8)
                        mine = [near[at, k * width : (k + 1) * width] for k in range(rows)]
                        dx, dy, dz = (mine[k] - other[k] for k in range(3))
                        inverse = lax.rsqrt(dx * dx + dy * dy + dz * dz + core_sq)
                        squared = inverse * inverse
                        burg_dot = mine[3] * other[3] + mine[4] * other[4] + mine[5] * other[5]
                        line_dot = mine[6] * other[6] + mine[7] * other[7] + mine[8] * other[8]
                        burg_own = mine[3] * dx + mine[4] * dy + mine[5] * dz
                        burg_far = other[3] * dx + other[4] * dy + other[5] * dz
                        weight = (line_dot * (squared * inverse)) * (
                            burg_dot - (3.0 * squared) * (burg_own * burg_far)
                        )
                        to = pl.ds(pl.multiple_of(sum_at + t, 8), 8)
                        total[0, to, :] += weight * dx
                        total[1, to, :] += weight * dy
                        total[2, to, :] += weight * dz

                return carry

            return lax.fori_loop(0, partners, one_partner, carry)

        lax.fori_loop(0, count, one_block, 0)
        ones = jnp.ones((8, width), jnp.bfloat16)
        dims = (((1,), (1,)), ((), ()))
        for k in range(3):
            high, low = halves(total[k])
            summed = lax.dot_general(ones, high, dims, preferred_element_type=jnp.float32) + lax.dot_general(
                ones, low, dims, preferred_element_type=jnp.float32
            )
            for b in range(count):
                out_ref[k, b : b + 1, :] = pair_scale * summed[0:1, b * width : (b + 1) * width]

    return pl.pallas_call(
        kernel,
        in_specs=[whole(pltpu.SMEM)] * 2 + [whole()] * 2 + anywhere(len(after)),
        out_specs=whole(),
        out_shape=jax.ShapeDtypeStruct((3, count, width), jnp.float32),
        scratch_shapes=[pltpu.VMEM((3, count * width, width), jnp.float32)],
        compiler_params=params(),
        cost_estimate=counted(cost),
        name="pair_pull",
    )(pairs, marks, near, far, *after)


def hint(name, index):
    costs = COSTS.get(name, ())
    return costs[index] if index < len(costs) else 0.0


def per_device(eigen, seg_vec, seg_off, seg_cell, blk_count, pair_list):
    plane_x, plane_y, length = eigen.shape
    groups_x = lax.axis_size("gx")
    groups_y = lax.axis_size("gy")
    per = length // groups_y
    sizes = CHUNKS if sum(CHUNKS) == per else (per,)
    offsets = [sum(sizes[:c]) for c in range(len(sizes))]
    chunks = len(sizes)
    place_x = lax.axis_index("gx").astype(jnp.int32)
    place_y = lax.axis_index("gy").astype(jnp.int32)
    me = jnp.stack([place_y, place_x])
    table = jnp.asarray(hartley_table(length))
    lines = jnp.asarray(line_tables(length, plane_x))

    def swap(parts):
        return [parts[0]] + [
            lax.ppermute(parts[d], "gy", [(i, i ^ d) for i in range(groups_y)])
            for d in range(1, groups_y)
        ]

    field = eigen.reshape(plane_x * plane_y, length)
    sent = [z_forward(field, table, me, groups_y, 0, sizes[0], [], hint("z_forward", 0))]

    seg_total = seg_cell.shape[2]
    block_total = blk_count.shape[2]
    width = seg_total // block_total
    cells = seg_cell.reshape(block_total, width)
    source, pairs = segment_rows(
        seg_vec.reshape(6, block_total, width),
        seg_off.reshape(3, block_total, width),
        cells,
        blk_count.reshape(block_total),
        pair_list.reshape(block_total, pair_list.shape[3]),
        me,
        plane_y,
        length,
        sent[0][0],
        hint("segment_rows", 0),
    )
    for c in range(1, chunks):
        sent.append(z_forward(field, table, me, groups_y, offsets[c], sizes[c], [source], hint("z_forward", c)))
    arrived = [swap(parts) for parts in sent]
    low = lax.ppermute(source, "gx", [(i, (i + 1) % groups_x) for i in range(groups_x)])
    high = lax.ppermute(source, "gx", [((i + 1) % groups_x, i) for i in range(groups_x)])

    near = spread_rows(source, [sent[-1][0]] if "near" in ORDER else [], hint("spread_rows", 0))

    levels = groups_x.bit_length() - 1
    forward, others, joined = [], [], []
    for c in range(chunks):
        after = [low, high, near] if c == 0 else [joined[0][-1] if "yf1" in ORDER else forward[-1][1]]
        forward.append(y_forward(arrived[c], table, lines, me, offsets[c], sizes[c], plane_x, plane_y, after, hint("y_forward", c)))
        others.append([])
        joined.append([forward[c][1]])
        for level in range(levels):
            others[c].append(lax.ppermute(joined[c][-1], "gx", [(i, i ^ 2**level) for i in range(groups_x)]))
            if level < levels - 1:
                joined[c].append(
                    join_ends(joined[c][-1], others[c][-1], forward[c][2], me, level, plane_x, [], hint("join_ends", 2 * c + level))
                )
    trio = join_rows(low, source, high, joined[0][-1] if "trio" in ORDER else forward[-1][1], hint("join_rows", 0))
    other = [(i, (i + 1 if i % 2 else i - 1) % groups_y) for i in range(groups_y)]
    trios = [
        trio,
        lax.ppermute(trio, "gy", [(i, i ^ 1) for i in range(groups_y)]),
        lax.ppermute(trio, "gy", other),
    ]
    far, marks = gather_rows(trios, me, plane_x, plane_y, hint("gather_rows", 0))

    shares = SHARES if len(SHARES) == chunks and sum(SHARES) == block_total else (0,) * (chunks - 1) + (block_total,)
    returned, pulls = [], []
    for c in range(chunks):
        spec, ends, own_lines = forward[c]
        after = pulls[-1:] if pulls else [far] + (joined[-1][-1:] if "yb0" in ORDER else [])
        returned.append(y_backward(spec, ends, others[c], table, own_lines, me, groups_y, plane_y, after, hint("y_backward", c)))
        first = sum(shares[:c])
        if shares[c]:
            pulls.append(pair_pull(near, far, marks, pairs, first, shares[c], returned[-1][:1], hint("pair_pull", c)))
    landed = [swap(parts) for parts in returned]

    pull = pulls[0] if len(pulls) == 1 else jnp.concatenate(pulls, axis=1)
    before = None
    flat_cells = seg_cell.reshape(1, seg_total)
    for c in range(chunks):
        before = z_backward(
            landed[c], table, flat_cells, me, groups_y, offsets[c], sizes[c], before,
            pull if c == chunks - 1 else None, source, pulls[-1:], hint("z_backward", c),
        )
    stress, force = before
    return stress.reshape(eigen.shape), force.reshape(3, 1, 1, seg_total)


def solution(mesh):
    return jax.shard_map(
        per_device,
        mesh=mesh,
        in_specs=(
            P("gx", "gy", None),
            P(None, "gx", "gy", None),
            P(None, "gx", "gy", None),
            P("gx", "gy", None),
            P("gx", "gy", None),
            P("gx", "gy", None, None),
        ),
        out_specs=(P("gx", "gy", None), P(None, "gx", "gy", None)),
        check_vma=False,
    )
```

```python
import math

import jax
import jax.numpy as jnp
import numpy as np
from jax import lax
from jax.experimental import pallas as pl
from jax.experimental.pallas import tpu as pltpu
from jax.sharding import PartitionSpec as P

nu_copper = 0.34
core_sq = 4.0
pair_scale = 4.0
CHUNKS = (32, 32)
SHARES = (5, 11)
ORDER = ()
VMEM_LIMIT = 24 * 1024 * 1024
COSTS = {'join_ends': (0, 3.0, 0, 2.0), 'pair_pull': (1.5, 0.0)}


def counted(cost):
    return pl.CostEstimate(flops=int(cost * 1e9), bytes_accessed=0, transcendentals=0)


def hartley_table(length):
    phase = np.outer(np.arange(length), np.arange(length)) % length
    angle = phase * (2.0 * math.pi / length)
    return ((np.cos(angle) + np.sin(angle)) / math.sqrt(length)).astype(np.float32)


def line_tables(length, plane_x):
    freq = np.arange(length, dtype=np.float64)
    wave = (2.0 * np.sin(math.pi * freq / length)) ** 2
    wave_z = wave[:, None]
    wave_y = wave[None, :]
    total = wave_y + wave_z
    zero = total == 0.0
    safe = np.where(zero, 1.0, total)
    ratio = 1.0 / (1.0 + safe / 2.0 + np.sqrt(safe + safe * safe / 4.0))
    ratio = ratio.astype(np.float32).astype(np.float64)
    elastic = 2.0 / (1.0 - nu_copper)
    gap = 1.0 - ratio * ratio
    green = ratio / gap
    first = -2.0 * (wave_y + elastic * wave_z) * green
    second = 2.0 * elastic * wave_z * safe * green * green
    weight_two = second
    weight_one = first + second * 2.0 * ratio * ratio / gap
    weight_zero = -first - second * (1.0 + ratio * ratio) / gap
    lap = ratio**length
    wrap_one = 1.0 / (1.0 - lap)
    wrap_two = length * lap / (1.0 - lap) ** 2
    leap = ratio**plane_x
    mask = np.where(zero, 0.0, 1.0)
    ratio = np.where(zero, 1.0, ratio)
    leap = np.where(zero, 1.0, leap)
    weight_zero = np.where(zero, 0.0, weight_zero)
    weight_one = np.where(zero, -1.0 / length, weight_one)
    weight_two = np.where(zero, 0.0, weight_two)
    wrap_one = np.where(zero, 1.0, wrap_one)
    wrap_two = np.where(zero, 0.0, wrap_two)
    tables = [ratio, leap, mask, weight_zero, weight_one, weight_two, wrap_one, wrap_two]
    return np.stack([t.astype(np.float32) for t in tables])


def halves(value):
    high = value.astype(jnp.bfloat16)
    low = (value - high.astype(jnp.float32)).astype(jnp.bfloat16)
    return high, low


def three_dots(left, right, dims):
    def one(a, b):
        return lax.dot_general(a, b, (dims, ((), ())), preferred_element_type=jnp.float32)

    return one(left[0], right[0]) + one(left[0], right[1]) + one(left[1], right[0])


def whole(memory=pltpu.VMEM):
    return pl.BlockSpec(memory_space=memory)


def anywhere(count):
    return [pl.BlockSpec(memory_space=pl.ANY)] * count


def params():
    return pltpu.CompilerParams(vmem_limit_bytes=VMEM_LIMIT)


def z_forward(field, table, me, groups, offset, rows, after, cost):
    cells, length = field.shape
    per = length // groups
    depth = groups * rows

    def kernel(me_ref, field_ref, table_ref, *refs):
        outs = refs[-groups:]
        own = me_ref[0]
        picked = [
            table_ref[pl.ds(pl.multiple_of((own ^ d) * per + offset, 8), rows), :] for d in range(groups)
        ]
        left = halves(jnp.concatenate(picked, axis=0))
        right = halves(field_ref[...])
        dims = (((1,), (1,)), ((), ()))
        both = lax.dot_general(
            jnp.concatenate(left, axis=0), right[0], dims, preferred_element_type=jnp.float32
        )
        result = both[:depth] + both[depth:]
        result = result + lax.dot_general(left[0], right[1], dims, preferred_element_type=jnp.float32)
        for d in range(groups):
            outs[d][...] = result[d * rows : (d + 1) * rows]

    return pl.pallas_call(
        kernel,
        in_specs=[whole(pltpu.SMEM)] + [whole()] * 2 + anywhere(len(after)),
        out_specs=[whole()] * groups,
        out_shape=[jax.ShapeDtypeStruct((rows, cells), jnp.float32)] * groups,
        compiler_params=params(),
        cost_estimate=counted(cost),
        name="z_forward",
    )(me, field, table, *after)


def y_rows(table_ref, own, groups, plane_y):
    picked = [
        table_ref[pl.ds(pl.multiple_of((own ^ d) * plane_y, 8), plane_y), :] for d in range(groups)
    ]
    return halves(jnp.concatenate(picked, axis=0))


def y_forward(parts, table, lines, me, offset, rows, plane_x, plane_y, after, cost):
    groups = len(parts)
    length = table.shape[0]
    per = length // groups

    def kernel(me_ref, *refs):
        part_refs = refs[:groups]
        table_ref, all_lines = refs[groups : groups + 2]
        spec_ref, ends_ref, lines_ref, gathered, lines_sem = refs[-5:]
        own = me_ref[0]
        first = pl.multiple_of(own * per + offset, 8)
        fetch = pltpu.make_async_copy(all_lines.at[:, pl.ds(first, rows)], lines_ref, lines_sem)
        fetch.start()
        right = y_rows(table_ref, own, groups, plane_y)
        for x in range(plane_x):
            gathered[x * rows : (x + 1) * rows, :] = jnp.concatenate(
                [ref[:, x * plane_y : (x + 1) * plane_y] for ref in part_refs], axis=1
            )
        result = three_dots(halves(gathered[...]), right, ((1,), (0,)))
        gathered[...] = result
        fetch.wait()
        ratio = lines_ref[0]
        mask = lines_ref[2]
        for g in range(0, rows, 8):
            step = ratio[g : g + 8]
            keep = mask[g : g + 8]
            zero = jnp.zeros_like(step)
            one, two = zero, zero
            for x in range(plane_x):
                value = gathered[x * rows + g : x * rows + g + 8, :]
                one = value + step * one
                two = one + step * two
                spec_ref[x, g : g + 8, :] = value * keep
            ends_ref[0, g : g + 8, :] = one
            ends_ref[1, g : g + 8, :] = two
            one, two = zero, zero
            for x in reversed(range(plane_x)):
                value = gathered[x * rows + g : x * rows + g + 8, :]
                one = value + step * one
                two = one + step * two
            ends_ref[2, g : g + 8, :] = one
            ends_ref[3, g : g + 8, :] = two

    return pl.pallas_call(
        kernel,
        in_specs=[whole(pltpu.SMEM)] + [whole()] * (groups + 1) + anywhere(1 + len(after)),
        out_specs=[whole()] * 3,
        out_shape=[
            jax.ShapeDtypeStruct((plane_x, rows, length), jnp.float32),
            jax.ShapeDtypeStruct((4, rows, length), jnp.float32),
            jax.ShapeDtypeStruct((lines.shape[0], rows, length), jnp.float32),
        ],
        scratch_shapes=[pltpu.VMEM((plane_x * rows, length), jnp.float32), pltpu.SemaphoreType.DMA],
        compiler_params=params(),
        cost_estimate=counted(cost),
        name="y_forward",
    )(me, *parts, table, lines, *after)


def leap_power(leap, exponent, top):
    result, factor, bit = None, leap, 1
    while bit < top:
        term = jnp.where((exponent & bit) != 0, factor, jnp.ones_like(factor))
        result = term if result is None else result * term
        factor = factor * factor
        bit *= 2
    return result


def join_ends(ends, other, lines, me, level, plane_x, after, cost):
    rows, length = ends.shape[1:]

    def kernel(me_ref, ends_ref, other_ref, lines_ref, *refs):
        out_ref = refs[-1]
        right_half = ((me_ref[1] >> level) & 1) == 1
        leap = lines_ref[1]
        for _ in range(level):
            leap = leap * leap
        span = float(plane_x * 2**level)
        for side in (0, 1):
            mine = [ends_ref[2 * side + k] for k in range(2)]
            theirs = [other_ref[2 * side + k] for k in range(2)]
            nearest = right_half if side == 0 else jnp.logical_not(right_half)
            near = [jnp.where(nearest, mine[k], theirs[k]) for k in range(2)]
            away = [jnp.where(nearest, theirs[k], mine[k]) for k in range(2)]
            out_ref[2 * side] = near[0] + leap * away[0]
            out_ref[2 * side + 1] = near[1] + leap * (away[1] + span * away[0])

    return pl.pallas_call(
        kernel,
        in_specs=[whole(pltpu.SMEM)] + [whole()] * 3 + anywhere(len(after)),
        out_specs=whole(),
        out_shape=jax.ShapeDtypeStruct(ends.shape, jnp.float32),
        compiler_params=params(),
        cost_estimate=counted(cost),
        name="join_ends",
    )(me, ends, other, lines, *after)


def y_backward(spec, ends, others, table, lines, me, groups, plane_y, after, cost):
    plane_x, rows, length = spec.shape
    levels = len(others)
    blocks = 2**levels

    def kernel(me_ref, spec_ref, ends_ref, *refs):
        other_refs = refs[:levels]
        table_ref, lines_ref = refs[levels : levels + 2]
        outs, work = refs[-1 - groups : -1], refs[-1]
        right = y_rows(table_ref, me_ref[0], groups, plane_y)
        place = me_ref[1]
        gaps = ([], [])
        for level in range(levels):
            size = 2**level
            inside = place & (size - 1)
            on_right = ((place >> level) & 1) == 1
            wrap = blocks - 2 * size
            gaps[0].append(inside + jnp.where(on_right, 0, wrap))
            gaps[1].append(size - 1 - inside + jnp.where(on_right, wrap, 0))
        for g in range(0, rows, 8):
            at = slice(g, g + 8)
            step, leap = lines_ref[0, at, :], lines_ref[1, at, :]
            wrap_one, wrap_two = lines_ref[6, at, :], lines_ref[7, at, :]
            power = jnp.ones_like(leap)
            for _ in range(blocks - 1):
                power = power * leap
            carries = []
            for side in (0, 1):
                far_one = ends_ref[2 * side, g : g + 8, :]
                far_two = ends_ref[2 * side + 1, g : g + 8, :]
                one = power * far_one
                two = power * (far_two + float(plane_x * (blocks - 1)) * far_one)
                for level in range(levels):
                    gap = gaps[side][level]
                    factor = leap_power(leap, gap, blocks)
                    far_one = other_refs[level][2 * side, g : g + 8, :]
                    far_two = other_refs[level][2 * side + 1, g : g + 8, :]
                    one = one + factor * far_one
                    two = two + factor * (far_two + (plane_x * gap).astype(jnp.float32) * far_one)
                carries.append((one * wrap_one, two * wrap_one + wrap_two * one))
            weight_zero, weight_one, weight_two = lines_ref[3, at, :], lines_ref[4, at, :], lines_ref[5, at, :]
            one, two = carries[0]
            for x in range(plane_x):
                value = spec_ref[x, g : g + 8, :]
                one = value + step * one
                two = one + step * two
                work[x * rows + g : x * rows + g + 8, :] = (
                    weight_zero * value + weight_one * one + weight_two * two
                )
            one, two = carries[1]
            for x in reversed(range(plane_x)):
                value = spec_ref[x, g : g + 8, :]
                one = value + step * one
                two = one + step * two
                work[x * rows + g : x * rows + g + 8, :] += weight_one * one + weight_two * two
        work[...] = three_dots(halves(work[...]), right, ((1,), (1,)))
        pack = max(1, 128 // plane_y)
        for x in range(0, plane_x, pack):
            for d in range(groups):
                outs[d][:, x * plane_y : (x + pack) * plane_y] = jnp.concatenate(
                    [
                        work[(x + k) * rows : (x + k + 1) * rows, d * plane_y : (d + 1) * plane_y]
                        for k in range(pack)
                    ],
                    axis=1,
                )

    return pl.pallas_call(
        kernel,
        in_specs=[whole(pltpu.SMEM)] + [whole()] * (levels + 4) + anywhere(len(after)),
        out_specs=[whole()] * groups,
        out_shape=[jax.ShapeDtypeStruct((rows, plane_x * plane_y), jnp.float32)] * groups,
        scratch_shapes=[pltpu.VMEM((plane_x * rows, length), jnp.float32)],
        compiler_params=params(),
        cost_estimate=counted(cost),
        name="y_backward",
    )(me, spec, ends, *others, table, lines, *after)


def segment_rows(vectors, offsets, cells, counts, pairs, me, plane_y, length, after, cost):
    blocks, width = cells.shape

    def kernel(counts_ref, me_ref, vectors_ref, offsets_ref, cells_ref, pairs_ref, after_ref, out_ref, places_ref):
        cell = cells_ref[...]
        out_ref[0] = (cell // (length * plane_y)).astype(jnp.float32) + offsets_ref[0]
        out_ref[1] = (cell // length % plane_y).astype(jnp.float32) + offsets_ref[1]
        out_ref[2] = (cell % length).astype(jnp.float32) + offsets_ref[2]
        lane = lax.broadcasted_iota(jnp.int32, (1, width), 1)
        for b in range(blocks):
            live = lane < counts_ref[b]
            for k in range(3):
                out_ref[3 + k, b : b + 1, :] = jnp.where(live, vectors_ref[k, b : b + 1, :], 0.0)
        for k in range(3):
            out_ref[6 + k] = vectors_ref[3 + k]
        number = pairs_ref[...]
        column = number // blocks % 3
        even = jnp.full_like(number, me_ref[0]) & 1 == 0
        slot = jnp.where(column == 1, 0, jnp.where((column == 2) == even, 1, 2))
        places_ref[...] = (slot * 3 + number // (3 * blocks)) * blocks + number % blocks

    return pl.pallas_call(
        kernel,
        in_specs=[whole(pltpu.SMEM)] * 2 + [whole()] * 4 + [pl.BlockSpec(memory_space=pl.ANY)],
        out_specs=[whole()] * 2,
        out_shape=[
            jax.ShapeDtypeStruct((9, blocks, width), jnp.float32),
            jax.ShapeDtypeStruct(pairs.shape, jnp.int32),
        ],
        compiler_params=params(),
        cost_estimate=counted(cost),
        name="segment_rows",
    )(counts, me, vectors, offsets, cells, pairs, after)


def sample_factors(cells, table, me, groups, offsets, sizes, cost):
    length = table.shape[0]
    per = length // groups
    seg_total = cells.shape[1]

    def kernel(me_ref, table_ref, cells_ref, *outs):
        own = me_ref[0]
        level = cells_ref[...] % length
        hot_z = jnp.where(
            lax.broadcasted_iota(jnp.int32, (length, seg_total), 0) == level, 1.0, 0.0
        ).astype(jnp.bfloat16)
        for out, offset, rows in zip(outs, offsets, sizes):
            picked = [
                table_ref[pl.ds(pl.multiple_of((own ^ d) * per + offset, 8), rows), :] for d in range(groups)
            ]
            right = jnp.concatenate(halves(jnp.concatenate(picked, axis=0)), axis=0)
            factor = jnp.dot(right, hot_z, preferred_element_type=jnp.float32)
            out[...] = factor[: groups * rows] + factor[groups * rows :]

    return pl.pallas_call(
        kernel,
        in_specs=[whole(pltpu.SMEM)] + [whole()] * 2,
        out_specs=[whole()] * len(sizes),
        out_shape=[jax.ShapeDtypeStruct((groups * rows, seg_total), jnp.float32) for rows in sizes],
        compiler_params=params(),
        cost_estimate=counted(cost),
        name="sample_factors",
    )(me, table, cells)


def z_backward(parts, table, cells, factor, me, groups, offset, rows, before, pull, source, after, cost):
    cell_total = parts[0].shape[1]
    length = table.shape[0]
    per = length // groups
    depth = groups * rows
    seg_total = cells.shape[1]
    blocks, width = source.shape[1:]
    tile = min(512, cell_total)
    steps = cell_total // tile
    adds = before is not None
    last = pull is not None

    def kernel(me_ref, *refs):
        part_refs, refs = refs[:groups], refs[groups:]
        table_ref, cells_ref, factor_ref, source_ref, refs = refs[0], refs[1], refs[2], refs[3], refs[4:]
        if adds:
            old_ref, old_tau_ref, refs = refs[0], refs[1], refs[2:]
        if last:
            pull_ref, refs = refs[0], refs[1:]
            stress_ref, out_ref, field, sems = refs[-4:]
        else:
            field, out_ref = refs[-2:]
        own = me_ref[0]
        picked = [
            table_ref[pl.ds(pl.multiple_of((own ^ d) * per + offset, 8), rows), :]
            for d in range(groups)
        ]
        right = halves(jnp.concatenate(picked, axis=0))
        left = halves(jnp.concatenate([ref[...] for ref in part_refs], axis=0))
        both = jnp.concatenate(left, axis=0)
        twice = jnp.concatenate([right[0], right[0]], axis=0)
        writes = []
        for i in range(steps):
            at = slice(i * tile, (i + 1) * tile)
            share = lax.dot_general(
                both[:, at], twice, (((0,), (0,)), ((), ())), preferred_element_type=jnp.float32
            ) + lax.dot_general(
                left[0][:, at], right[1], (((0,), (0,)), ((), ())), preferred_element_type=jnp.float32
            )
            field[at, :] = share + old_ref[at, :] if adds else share
            if last:
                writes.append(
                    pltpu.make_async_copy(
                        field.at[pl.ds(i * tile, tile)], stress_ref.at[pl.ds(i * tile, tile)], sems.at[i]
                    )
                )
                writes[-1].start()
        place = cells_ref[...] // length
        lane_tile = min(512, seg_total)
        taus = []
        for k in range(0, seg_total, lane_tile):
            at = slice(k, k + lane_tile)
            hot = jnp.where(
                lax.broadcasted_iota(jnp.int32, (cell_total, lane_tile), 0) == place[:, at], 1.0, 0.0
            ).astype(jnp.bfloat16)
            found = jnp.dot(both, hot, preferred_element_type=jnp.float32)
            tau = jnp.sum((found[:depth] + found[depth:]) * factor_ref[:, at], axis=0, keepdims=True)
            taus += [tau[:, j : j + width] for j in range(0, lane_tile, width)]
        tau = jnp.concatenate(taus, axis=0)
        if adds:
            tau = tau + old_tau_ref[...]
        if last:
            b0, b1, b2, t0, t1, t2 = (source_ref[3 + k] for k in range(6))
            out_ref[0] = pull_ref[0] + tau * (b1 * t2 - b2 * t1)
            out_ref[1] = pull_ref[1] + tau * (b2 * t0 - b0 * t2)
            out_ref[2] = pull_ref[2] + tau * (b0 * t1 - b1 * t0)
        else:
            out_ref[...] = tau
        for write in writes:
            write.wait()

    operands = [me, *parts, table, cells, factor, source]
    if adds:
        operands += list(before)
    if last:
        operands.append(pull)
    scratch = [pltpu.VMEM((cell_total, length), jnp.float32), pltpu.SemaphoreType.DMA((steps,))]
    return pl.pallas_call(
        kernel,
        in_specs=[whole(pltpu.SMEM)] + [whole()] * (len(operands) - 1) + anywhere(len(after)),
        out_specs=(anywhere(1) if last else [whole()]) + [whole()],
        out_shape=[
            jax.ShapeDtypeStruct((cell_total, length), jnp.float32),
            jax.ShapeDtypeStruct((3, blocks, width) if last else (blocks, width), jnp.float32),
        ],
        scratch_shapes=scratch if last else [],
        compiler_params=params(),
        cost_estimate=counted(cost),
        name="z_backward",
    )(*operands, *after)


def join_rows(low, own, high, after, cost):
    rows = own.shape[0]

    def kernel(low_ref, own_ref, high_ref, after_ref, out_ref):
        out_ref[0:rows] = low_ref[...]
        out_ref[rows : 2 * rows] = own_ref[...]
        out_ref[2 * rows :] = high_ref[...]

    return pl.pallas_call(
        kernel,
        in_specs=[whole()] * 3 + anywhere(1),
        out_specs=whole(),
        out_shape=jax.ShapeDtypeStruct((3 * rows,) + own.shape[1:], jnp.float32),
        compiler_params=params(),
        cost_estimate=counted(cost),
        name="join_rows",
    )(low, own, high, after)


def spread_rows(source, after, cost):
    rows, blocks, width = source.shape

    def kernel(source_ref, *refs):
        near = refs[-1]
        spread_row = lax.broadcasted_iota(jnp.int32, (3 * rows, rows * width), 0) % rows
        spread_col = lax.broadcasted_iota(jnp.int32, (3 * rows, rows * width), 1) // width
        spread = (spread_row == spread_col).astype(jnp.bfloat16)
        for b in range(blocks):
            own = jnp.concatenate([source_ref[k, b : b + 1, :] for k in range(rows)], axis=0)
            high = own.astype(jnp.bfloat16).astype(jnp.float32)
            rest = own - high
            middle = rest.astype(jnp.bfloat16).astype(jnp.float32)
            split = jnp.concatenate([high, middle, rest - middle], axis=0).astype(jnp.bfloat16)
            near[b * width : (b + 1) * width, :] = lax.dot_general(
                split, spread, (((0,), (0,)), ((), ())), preferred_element_type=jnp.float32
            )

    return pl.pallas_call(
        kernel,
        in_specs=[whole()] + anywhere(len(after)),
        out_specs=whole(),
        out_shape=jax.ShapeDtypeStruct((blocks * width, rows * width), jnp.float32),
        compiler_params=params(),
        cost_estimate=counted(cost),
        name="spread_rows",
    )(source, *after)


def gather_rows(trios, me, plane_x, plane_y, cost):
    blocks, width = trios[0].shape[1:]
    rows = trios[0].shape[0] // 3
    stride = rows * blocks
    padded = (9 * blocks + 127) // 128 * 128

    def kernel(me_ref, *refs):
        trio_refs = refs[:3]
        far, marks, flags = refs[3:]
        toward = jnp.where(me_ref[0] & 1 == 1, -float(plane_y), float(plane_y))
        flags[...] = jnp.zeros_like(flags)
        for slot in range(3):
            for p in range(3):
                base = slot * 3 + p
                trio = trio_refs[slot]
                for k in range(rows):
                    value = trio[p * rows + k]
                    if k == 0 and p != 1:
                        value = value + float((p - 1) * plane_x)
                    if k == 1 and slot > 0:
                        value = value + (toward if slot == 1 else -toward)
                    at = base * stride + k * blocks
                    far[at : at + blocks, :] = value
                size = jnp.maximum(
                    jnp.maximum(jnp.abs(trio[p * rows + 3]), jnp.abs(trio[p * rows + 4])),
                    jnp.abs(trio[p * rows + 5]),
                )
                flags[base * blocks : (base + 1) * blocks, :] = (size > 0.0).astype(jnp.float32)
        marks[...] = lax.dot_general(
            jnp.ones((8, width), jnp.bfloat16),
            flags[...].astype(jnp.bfloat16),
            (((1,), (1,)), ((), ())),
            preferred_element_type=jnp.float32,
        ).astype(jnp.int32)

    return pl.pallas_call(
        kernel,
        in_specs=[whole(pltpu.SMEM)] + [whole()] * 3,
        out_specs=[whole()] * 2,
        out_shape=[
            jax.ShapeDtypeStruct((9 * stride, width), jnp.float32),
            jax.ShapeDtypeStruct((8, padded), jnp.int32),
        ],
        scratch_shapes=[pltpu.VMEM((padded, width), jnp.float32)],
        compiler_params=params(),
        cost_estimate=counted(cost),
        name="gather_rows",
    )(me, *trios)


def pair_pull(near, far, marks, pairs, first_block, count, after, cost):
    blocks, partners = pairs.shape
    width = near.shape[0] // blocks
    rows = near.shape[1] // width
    stride = rows * blocks

    def kernel(pairs_ref, marks_ref, near, far, *refs):
        out_ref, total = refs[-2:]
        total[...] = jnp.zeros_like(total)

        def one_block(index, carry):
            b = first_block + index
            own_at = pl.multiple_of(b * width, width)
            sum_at = pl.multiple_of(index * width, width)

            def one_partner(p, carry):
                number = pairs_ref[b, p]

                @pl.when(marks_ref[0, number] > 0)
                def _():
                    first = number // blocks * stride + number % blocks
                    other = [
                        jnp.broadcast_to(far[pl.ds(first + k * blocks, 1), :], (8, width)) for k in range(rows)
                    ]
                    for t in range(0, width, 8):
                        at = pl.ds(pl.multiple_of(own_at + t, 8), 8)
                        mine = [near[at, k * width : (k + 1) * width] for k in range(rows)]
                        dx, dy, dz = (mine[k] - other[k] for k in range(3))
                        inverse = lax.rsqrt(dx * dx + dy * dy + dz * dz + core_sq)
                        squared = inverse * inverse
                        burg_dot = mine[3] * other[3] + mine[4] * other[4] + mine[5] * other[5]
                        line_dot = mine[6] * other[6] + mine[7] * other[7] + mine[8] * other[8]
                        burg_own = mine[3] * dx + mine[4] * dy + mine[5] * dz
                        burg_far = other[3] * dx + other[4] * dy + other[5] * dz
                        weight = (line_dot * (squared * inverse)) * (
                            burg_dot - (3.0 * squared) * (burg_own * burg_far)
                        )
                        to = pl.ds(pl.multiple_of(sum_at + t, 8), 8)
                        total[0, to, :] += weight * dx
                        total[1, to, :] += weight * dy
                        total[2, to, :] += weight * dz

                return carry

            return lax.fori_loop(0, partners, one_partner, carry)

        lax.fori_loop(0, count, one_block, 0)
        ones = jnp.ones((8, width), jnp.bfloat16)
        dims = (((1,), (1,)), ((), ()))
        for k in range(3):
            high, low = halves(total[k])
            summed = lax.dot_general(ones, high, dims, preferred_element_type=jnp.float32) + lax.dot_general(
                ones, low, dims, preferred_element_type=jnp.float32
            )
            for b in range(count):
                out_ref[k, b : b + 1, :] = pair_scale * summed[0:1, b * width : (b + 1) * width]

    return pl.pallas_call(
        kernel,
        in_specs=[whole(pltpu.SMEM)] * 2 + [whole()] * 2 + anywhere(len(after)),
        out_specs=whole(),
        out_shape=jax.ShapeDtypeStruct((3, count, width), jnp.float32),
        scratch_shapes=[pltpu.VMEM((3, count * width, width), jnp.float32)],
        compiler_params=params(),
        cost_estimate=counted(cost),
        name="pair_pull",
    )(pairs, marks, near, far, *after)


def hint(name, index):
    costs = COSTS.get(name, ())
    return costs[index] if index < len(costs) else 0.0


def per_device(eigen, seg_vec, seg_off, seg_cell, blk_count, pair_list):
    plane_x, plane_y, length = eigen.shape
    groups_x = lax.axis_size("gx")
    groups_y = lax.axis_size("gy")
    per = length // groups_y
    sizes = CHUNKS if sum(CHUNKS) == per else (per,)
    offsets = [sum(sizes[:c]) for c in range(len(sizes))]
    chunks = len(sizes)
    place_x = lax.axis_index("gx").astype(jnp.int32)
    place_y = lax.axis_index("gy").astype(jnp.int32)
    me = jnp.stack([place_y, place_x])
    table = jnp.asarray(hartley_table(length))
    lines = jnp.asarray(line_tables(length, plane_x))

    def swap(parts):
        return [parts[0]] + [
            lax.ppermute(parts[d], "gy", [(i, i ^ d) for i in range(groups_y)])
            for d in range(1, groups_y)
        ]

    field = eigen.reshape(plane_x * plane_y, length)
    sent = [z_forward(field, table, me, groups_y, 0, sizes[0], [], hint("z_forward", 0))]

    seg_total = seg_cell.shape[2]
    block_total = blk_count.shape[2]
    width = seg_total // block_total
    cells = seg_cell.reshape(block_total, width)
    source, pairs = segment_rows(
        seg_vec.reshape(6, block_total, width),
        seg_off.reshape(3, block_total, width),
        cells,
        blk_count.reshape(block_total),
        pair_list.reshape(block_total, pair_list.shape[3]),
        me,
        plane_y,
        length,
        sent[0][0],
        hint("segment_rows", 0),
    )
    for c in range(1, chunks):
        sent.append(z_forward(field, table, me, groups_y, offsets[c], sizes[c], [source], hint("z_forward", c)))
    arrived = [swap(parts) for parts in sent]
    low = lax.ppermute(source, "gx", [(i, (i + 1) % groups_x) for i in range(groups_x)])
    high = lax.ppermute(source, "gx", [((i + 1) % groups_x, i) for i in range(groups_x)])

    near = spread_rows(source, [sent[-1][0]] if "near" in ORDER else [], hint("spread_rows", 0))
    flat_cells = seg_cell.reshape(1, seg_total)
    factors = sample_factors(flat_cells, table, me, groups_y, offsets, sizes, 0.0)

    levels = groups_x.bit_length() - 1
    forward, others, joined = [], [], []
    for c in range(chunks):
        after = [low, high, near, factors[0]] if c == 0 else [joined[0][-1] if "yf1" in ORDER else forward[-1][1]]
        forward.append(y_forward(arrived[c], table, lines, me, offsets[c], sizes[c], plane_x, plane_y, after, hint("y_forward", c)))
        others.append([])
        joined.append([forward[c][1]])
        for level in range(levels):
            others[c].append(lax.ppermute(joined[c][-1], "gx", [(i, i ^ 2**level) for i in range(groups_x)]))
            if level < levels - 1:
                joined[c].append(
                    join_ends(joined[c][-1], others[c][-1], forward[c][2], me, level, plane_x, [], hint("join_ends", 2 * c + level))
                )
    trio = join_rows(low, source, high, joined[0][-1] if "trio" in ORDER else forward[-1][1], hint("join_rows", 0))
    other = [(i, (i + 1 if i % 2 else i - 1) % groups_y) for i in range(groups_y)]
    trios = [
        trio,
        lax.ppermute(trio, "gy", [(i, i ^ 1) for i in range(groups_y)]),
        lax.ppermute(trio, "gy", other),
    ]
    far, marks = gather_rows(trios, me, plane_x, plane_y, hint("gather_rows", 0))

    shares = SHARES if len(SHARES) == chunks and sum(SHARES) == block_total else (0,) * (chunks - 1) + (block_total,)
    returned, pulls = [], []
    for c in range(chunks):
        spec, ends, own_lines = forward[c]
        after = pulls[-1:] if pulls else [far] + (joined[-1][-1:] if "yb0" in ORDER else [])
        returned.append(y_backward(spec, ends, others[c], table, own_lines, me, groups_y, plane_y, after, hint("y_backward", c)))
        first = sum(shares[:c])
        if shares[c]:
            pulls.append(pair_pull(near, far, marks, pairs, first, shares[c], returned[-1][:1], hint("pair_pull", c)))
    landed = [swap(parts) for parts in returned]

    pull = pulls[0] if len(pulls) == 1 else jnp.concatenate(pulls, axis=1)
    before = None
    for c in range(chunks):
        before = z_backward(
            landed[c], table, flat_cells, factors[c], me, groups_y, offsets[c], sizes[c], before,
            pull if c == chunks - 1 else None, source, pulls[-1:], hint("z_backward", c),
        )
    stress, force = before
    return stress.reshape(eigen.shape), force.reshape(3, 1, 1, seg_total)


def solution(mesh):
    return jax.shard_map(
        per_device,
        mesh=mesh,
        in_specs=(
            P("gx", "gy", None),
            P(None, "gx", "gy", None),
            P(None, "gx", "gy", None),
            P("gx", "gy", None),
            P("gx", "gy", None),
            P("gx", "gy", None, None),
        ),
        out_specs=(P("gx", "gy", None), P(None, "gx", "gy", None)),
        check_vma=False,
    )
```

```python
import math

import jax
import jax.numpy as jnp
import numpy as np
from jax import lax
from jax.experimental import pallas as pl
from jax.experimental.pallas import tpu as pltpu
from jax.sharding import PartitionSpec as P

nu_copper = 0.34
core_sq = 4.0
pair_scale = 4.0
CHUNKS = (32, 32)
SHARES = (5, 11)
ORDER = ()
VMEM_LIMIT = 24 * 1024 * 1024
COSTS = {'join_ends': (0, 3.0, 0, 2.0), 'pair_pull': (1.5, 0.0)}


def counted(cost):
    return pl.CostEstimate(flops=int(cost * 1e9), bytes_accessed=0, transcendentals=0)


def hartley_table(length):
    phase = np.outer(np.arange(length), np.arange(length)) % length
    angle = phase * (2.0 * math.pi / length)
    return ((np.cos(angle) + np.sin(angle)) / math.sqrt(length)).astype(np.float32)


def line_tables(length, plane_x):
    freq = np.arange(length, dtype=np.float64)
    wave = (2.0 * np.sin(math.pi * freq / length)) ** 2
    wave_z = wave[:, None]
    wave_y = wave[None, :]
    total = wave_y + wave_z
    zero = total == 0.0
    safe = np.where(zero, 1.0, total)
    ratio = 1.0 / (1.0 + safe / 2.0 + np.sqrt(safe + safe * safe / 4.0))
    ratio = ratio.astype(np.float32).astype(np.float64)
    elastic = 2.0 / (1.0 - nu_copper)
    gap = 1.0 - ratio * ratio
    green = ratio / gap
    first = -2.0 * (wave_y + elastic * wave_z) * green
    second = 2.0 * elastic * wave_z * safe * green * green
    weight_two = second
    weight_one = first + second * 2.0 * ratio * ratio / gap
    weight_zero = -first - second * (1.0 + ratio * ratio) / gap
    lap = ratio**length
    wrap_one = 1.0 / (1.0 - lap)
    wrap_two = length * lap / (1.0 - lap) ** 2
    leap = ratio**plane_x
    mask = np.where(zero, 0.0, 1.0)
    ratio = np.where(zero, 1.0, ratio)
    leap = np.where(zero, 1.0, leap)
    weight_zero = np.where(zero, 0.0, weight_zero)
    weight_one = np.where(zero, -1.0 / length, weight_one)
    weight_two = np.where(zero, 0.0, weight_two)
    wrap_one = np.where(zero, 1.0, wrap_one)
    wrap_two = np.where(zero, 0.0, wrap_two)
    tables = [ratio, leap, mask, weight_zero, weight_one, weight_two, wrap_one, wrap_two]
    return np.stack([t.astype(np.float32) for t in tables])


def halves(value):
    high = value.astype(jnp.bfloat16)
    low = (value - high.astype(jnp.float32)).astype(jnp.bfloat16)
    return high, low


def three_dots(left, right, dims):
    def one(a, b):
        return lax.dot_general(a, b, (dims, ((), ())), preferred_element_type=jnp.float32)

    rows = left[0].shape[0]
    both = one(jnp.concatenate(left, axis=0), right[0])
    return both[:rows] + both[rows:] + one(left[0], right[1])


def whole(memory=pltpu.VMEM):
    return pl.BlockSpec(memory_space=memory)


def anywhere(count):
    return [pl.BlockSpec(memory_space=pl.ANY)] * count


def params():
    return pltpu.CompilerParams(vmem_limit_bytes=VMEM_LIMIT)


def z_forward(field, table, me, groups, offset, rows, after, cost):
    cells, length = field.shape
    per = length // groups
    depth = groups * rows

    def kernel(me_ref, field_ref, table_ref, *refs):
        outs = refs[-groups:]
        own = me_ref[0]
        picked = [
            table_ref[pl.ds(pl.multiple_of((own ^ d) * per + offset, 8), rows), :] for d in range(groups)
        ]
        left = halves(jnp.concatenate(picked, axis=0))
        right = halves(field_ref[...])
        dims = (((1,), (1,)), ((), ()))
        both = lax.dot_general(
            jnp.concatenate(left, axis=0), right[0], dims, preferred_element_type=jnp.float32
        )
        result = both[:depth] + both[depth:]
        result = result + lax.dot_general(left[0], right[1], dims, preferred_element_type=jnp.float32)
        for d in range(groups):
            outs[d][...] = result[d * rows : (d + 1) * rows]

    return pl.pallas_call(
        kernel,
        in_specs=[whole(pltpu.SMEM)] + [whole()] * 2 + anywhere(len(after)),
        out_specs=[whole()] * groups,
        out_shape=[jax.ShapeDtypeStruct((rows, cells), jnp.float32)] * groups,
        compiler_params=params(),
        cost_estimate=counted(cost),
        name="z_forward",
    )(me, field, table, *after)


def y_rows(table_ref, own, groups, plane_y):
    picked = [
        table_ref[pl.ds(pl.multiple_of((own ^ d) * plane_y, 8), plane_y), :] for d in range(groups)
    ]
    return halves(jnp.concatenate(picked, axis=0))


def y_forward(parts, table, lines, me, offset, rows, plane_x, plane_y, after, cost):
    groups = len(parts)
    length = table.shape[0]
    per = length // groups

    def kernel(me_ref, *refs):
        part_refs = refs[:groups]
        table_ref, all_lines = refs[groups : groups + 2]
        spec_ref, ends_ref, lines_ref, gathered, lines_sem = refs[-5:]
        own = me_ref[0]
        first = pl.multiple_of(own * per + offset, 8)
        fetch = pltpu.make_async_copy(all_lines.at[:, pl.ds(first, rows)], lines_ref, lines_sem)
        fetch.start()
        right = y_rows(table_ref, own, groups, plane_y)
        for x in range(plane_x):
            gathered[x * rows : (x + 1) * rows, :] = jnp.concatenate(
                [ref[:, x * plane_y : (x + 1) * plane_y] for ref in part_refs], axis=1
            )
        result = three_dots(halves(gathered[...]), right, ((1,), (0,)))
        gathered[...] = result
        fetch.wait()
        ratio = lines_ref[0]
        mask = lines_ref[2]
        for g in range(0, rows, 8):
            step = ratio[g : g + 8]
            keep = mask[g : g + 8]
            zero = jnp.zeros_like(step)
            one, two = zero, zero
            for x in range(plane_x):
                value = gathered[x * rows + g : x * rows + g + 8, :]
                one = value + step * one
                two = one + step * two
                spec_ref[x, g : g + 8, :] = value * keep
            ends_ref[0, g : g + 8, :] = one
            ends_ref[1, g : g + 8, :] = two
            one, two = zero, zero
            for x in reversed(range(plane_x)):
                value = gathered[x * rows + g : x * rows + g + 8, :]
                one = value + step * one
                two = one + step * two
            ends_ref[2, g : g + 8, :] = one
            ends_ref[3, g : g + 8, :] = two

    return pl.pallas_call(
        kernel,
        in_specs=[whole(pltpu.SMEM)] + [whole()] * (groups + 1) + anywhere(1 + len(after)),
        out_specs=[whole()] * 3,
        out_shape=[
            jax.ShapeDtypeStruct((plane_x, rows, length), jnp.float32),
            jax.ShapeDtypeStruct((4, rows, length), jnp.float32),
            jax.ShapeDtypeStruct((lines.shape[0], rows, length), jnp.float32),
        ],
        scratch_shapes=[pltpu.VMEM((plane_x * rows, length), jnp.float32), pltpu.SemaphoreType.DMA],
        compiler_params=params(),
        cost_estimate=counted(cost),
        name="y_forward",
    )(me, *parts, table, lines, *after)


def leap_power(leap, exponent, top):
    result, factor, bit = None, leap, 1
    while bit < top:
        term = jnp.where((exponent & bit) != 0, factor, jnp.ones_like(factor))
        result = term if result is None else result * term
        factor = factor * factor
        bit *= 2
    return result


def join_ends(ends, other, lines, me, level, plane_x, after, cost):
    rows, length = ends.shape[1:]

    def kernel(me_ref, ends_ref, other_ref, lines_ref, *refs):
        out_ref = refs[-1]
        right_half = ((me_ref[1] >> level) & 1) == 1
        leap = lines_ref[1]
        for _ in range(level):
            leap = leap * leap
        span = float(plane_x * 2**level)
        for side in (0, 1):
            mine = [ends_ref[2 * side + k] for k in range(2)]
            theirs = [other_ref[2 * side + k] for k in range(2)]
            nearest = right_half if side == 0 else jnp.logical_not(right_half)
            near = [jnp.where(nearest, mine[k], theirs[k]) for k in range(2)]
            away = [jnp.where(nearest, theirs[k], mine[k]) for k in range(2)]
            out_ref[2 * side] = near[0] + leap * away[0]
            out_ref[2 * side + 1] = near[1] + leap * (away[1] + span * away[0])

    return pl.pallas_call(
        kernel,
        in_specs=[whole(pltpu.SMEM)] + [whole()] * 3 + anywhere(len(after)),
        out_specs=whole(),
        out_shape=jax.ShapeDtypeStruct(ends.shape, jnp.float32),
        compiler_params=params(),
        cost_estimate=counted(cost),
        name="join_ends",
    )(me, ends, other, lines, *after)


def y_backward(spec, ends, others, table, lines, me, groups, plane_y, after, cost):
    plane_x, rows, length = spec.shape
    levels = len(others)
    blocks = 2**levels

    def kernel(me_ref, spec_ref, ends_ref, *refs):
        other_refs = refs[:levels]
        table_ref, lines_ref = refs[levels : levels + 2]
        outs, work = refs[-1 - groups : -1], refs[-1]
        right = y_rows(table_ref, me_ref[0], groups, plane_y)
        place = me_ref[1]
        gaps = ([], [])
        for level in range(levels):
            size = 2**level
            inside = place & (size - 1)
            on_right = ((place >> level) & 1) == 1
            wrap = blocks - 2 * size
            gaps[0].append(inside + jnp.where(on_right, 0, wrap))
            gaps[1].append(size - 1 - inside + jnp.where(on_right, wrap, 0))
        for g in range(0, rows, 8):
            at = slice(g, g + 8)
            step, leap = lines_ref[0, at, :], lines_ref[1, at, :]
            wrap_one, wrap_two = lines_ref[6, at, :], lines_ref[7, at, :]
            power = jnp.ones_like(leap)
            for _ in range(blocks - 1):
                power = power * leap
            carries = []
            for side in (0, 1):
                far_one = ends_ref[2 * side, g : g + 8, :]
                far_two = ends_ref[2 * side + 1, g : g + 8, :]
                one = power * far_one
                two = power * (far_two + float(plane_x * (blocks - 1)) * far_one)
                for level in range(levels):
                    gap = gaps[side][level]
                    factor = leap_power(leap, gap, blocks)
                    far_one = other_refs[level][2 * side, g : g + 8, :]
                    far_two = other_refs[level][2 * side + 1, g : g + 8, :]
                    one = one + factor * far_one
                    two = two + factor * (far_two + (plane_x * gap).astype(jnp.float32) * far_one)
                carries.append((one * wrap_one, two * wrap_one + wrap_two * one))
            weight_zero, weight_one, weight_two = lines_ref[3, at, :], lines_ref[4, at, :], lines_ref[5, at, :]
            one, two = carries[0]
            for x in range(plane_x):
                value = spec_ref[x, g : g + 8, :]
                one = value + step * one
                two = one + step * two
                work[x * rows + g : x * rows + g + 8, :] = (
                    weight_zero * value + weight_one * one + weight_two * two
                )
            one, two = carries[1]
            for x in reversed(range(plane_x)):
                value = spec_ref[x, g : g + 8, :]
                one = value + step * one
                two = one + step * two
                work[x * rows + g : x * rows + g + 8, :] += weight_one * one + weight_two * two
        work[...] = three_dots(halves(work[...]), right, ((1,), (1,)))
        pack = max(1, 128 // plane_y)
        for x in range(0, plane_x, pack):
            for d in range(groups):
                outs[d][:, x * plane_y : (x + pack) * plane_y] = jnp.concatenate(
                    [
                        work[(x + k) * rows : (x + k + 1) * rows, d * plane_y : (d + 1) * plane_y]
                        for k in range(pack)
                    ],
                    axis=1,
                )

    return pl.pallas_call(
        kernel,
        in_specs=[whole(pltpu.SMEM)] + [whole()] * (levels + 4) + anywhere(len(after)),
        out_specs=[whole()] * groups,
        out_shape=[jax.ShapeDtypeStruct((rows, plane_x * plane_y), jnp.float32)] * groups,
        scratch_shapes=[pltpu.VMEM((plane_x * rows, length), jnp.float32)],
        compiler_params=params(),
        cost_estimate=counted(cost),
        name="y_backward",
    )(me, spec, ends, *others, table, lines, *after)


def segment_rows(vectors, offsets, cells, counts, pairs, me, plane_y, length, after, cost):
    blocks, width = cells.shape

    def kernel(counts_ref, me_ref, vectors_ref, offsets_ref, cells_ref, pairs_ref, after_ref, out_ref, places_ref):
        cell = cells_ref[...]
        out_ref[0] = (cell // (length * plane_y)).astype(jnp.float32) + offsets_ref[0]
        out_ref[1] = (cell // length % plane_y).astype(jnp.float32) + offsets_ref[1]
        out_ref[2] = (cell % length).astype(jnp.float32) + offsets_ref[2]
        lane = lax.broadcasted_iota(jnp.int32, (1, width), 1)
        for b in range(blocks):
            live = lane < counts_ref[b]
            for k in range(3):
                out_ref[3 + k, b : b + 1, :] = jnp.where(live, vectors_ref[k, b : b + 1, :], 0.0)
        for k in range(3):
            out_ref[6 + k] = vectors_ref[3 + k]
        number = pairs_ref[...]
        column = number // blocks % 3
        even = jnp.full_like(number, me_ref[0]) & 1 == 0
        slot = jnp.where(column == 1, 0, jnp.where((column == 2) == even, 1, 2))
        places_ref[...] = (slot * 3 + number // (3 * blocks)) * blocks + number % blocks

    return pl.pallas_call(
        kernel,
        in_specs=[whole(pltpu.SMEM)] * 2 + [whole()] * 4 + [pl.BlockSpec(memory_space=pl.ANY)],
        out_specs=[whole()] * 2,
        out_shape=[
            jax.ShapeDtypeStruct((9, blocks, width), jnp.float32),
            jax.ShapeDtypeStruct(pairs.shape, jnp.int32),
        ],
        compiler_params=params(),
        cost_estimate=counted(cost),
        name="segment_rows",
    )(counts, me, vectors, offsets, cells, pairs, after)


def sample_factors(cells, table, me, groups, offsets, sizes, cost):
    length = table.shape[0]
    per = length // groups
    seg_total = cells.shape[1]

    def kernel(me_ref, table_ref, cells_ref, *outs):
        own = me_ref[0]
        level = cells_ref[...] % length
        hot_z = jnp.where(
            lax.broadcasted_iota(jnp.int32, (length, seg_total), 0) == level, 1.0, 0.0
        ).astype(jnp.bfloat16)
        for out, offset, rows in zip(outs, offsets, sizes):
            picked = [
                table_ref[pl.ds(pl.multiple_of((own ^ d) * per + offset, 8), rows), :] for d in range(groups)
            ]
            right = jnp.concatenate(halves(jnp.concatenate(picked, axis=0)), axis=0)
            factor = jnp.dot(right, hot_z, preferred_element_type=jnp.float32)
            out[...] = factor[: groups * rows] + factor[groups * rows :]

    return pl.pallas_call(
        kernel,
        in_specs=[whole(pltpu.SMEM)] + [whole()] * 2,
        out_specs=[whole()] * len(sizes),
        out_shape=[jax.ShapeDtypeStruct((groups * rows, seg_total), jnp.float32) for rows in sizes],
        compiler_params=params(),
        cost_estimate=counted(cost),
        name="sample_factors",
    )(me, table, cells)


def z_backward(parts, table, cells, factor, me, groups, offset, rows, before, pull, source, after, cost):
    cell_total = parts[0].shape[1]
    length = table.shape[0]
    per = length // groups
    depth = groups * rows
    seg_total = cells.shape[1]
    blocks, width = source.shape[1:]
    tile = min(512, cell_total)
    steps = cell_total // tile
    adds = before is not None
    last = pull is not None

    def kernel(me_ref, *refs):
        part_refs, refs = refs[:groups], refs[groups:]
        table_ref, cells_ref, factor_ref, source_ref, refs = refs[0], refs[1], refs[2], refs[3], refs[4:]
        if adds:
            old_ref, old_tau_ref, refs = refs[0], refs[1], refs[2:]
        if last:
            pull_ref, refs = refs[0], refs[1:]
            stress_ref, out_ref, field, sems = refs[-4:]
        else:
            field, out_ref = refs[-2:]
        own = me_ref[0]
        picked = [
            table_ref[pl.ds(pl.multiple_of((own ^ d) * per + offset, 8), rows), :]
            for d in range(groups)
        ]
        right = halves(jnp.concatenate(picked, axis=0))
        left = halves(jnp.concatenate([ref[...] for ref in part_refs], axis=0))
        both = jnp.concatenate(left, axis=0)
        twice = jnp.concatenate([right[0], right[0]], axis=0)
        writes = []
        for i in range(steps):
            at = slice(i * tile, (i + 1) * tile)
            share = lax.dot_general(
                both[:, at], twice, (((0,), (0,)), ((), ())), preferred_element_type=jnp.float32
            ) + lax.dot_general(
                left[0][:, at], right[1], (((0,), (0,)), ((), ())), preferred_element_type=jnp.float32
            )
            field[at, :] = share + old_ref[at, :] if adds else share
            if last:
                writes.append(
                    pltpu.make_async_copy(
                        field.at[pl.ds(i * tile, tile)], stress_ref.at[pl.ds(i * tile, tile)], sems.at[i]
                    )
                )
                writes[-1].start()
        place = cells_ref[...] // length
        lane_tile = min(1024, seg_total)
        taus = []
        for k in range(0, seg_total, lane_tile):
            at = slice(k, k + lane_tile)
            hot = jnp.where(
                lax.broadcasted_iota(jnp.int32, (cell_total, lane_tile), 0) == place[:, at], 1.0, 0.0
            ).astype(jnp.bfloat16)
            found = jnp.dot(both, hot, preferred_element_type=jnp.float32)
            tau = jnp.sum((found[:depth] + found[depth:]) * factor_ref[:, at], axis=0, keepdims=True)
            taus += [tau[:, j : j + width] for j in range(0, lane_tile, width)]
        tau = jnp.concatenate(taus, axis=0)
        if adds:
            tau = tau + old_tau_ref[...]
        if last:
            b0, b1, b2, t0, t1, t2 = (source_ref[3 + k] for k in range(6))
            out_ref[0] = pull_ref[0] + tau * (b1 * t2 - b2 * t1)
            out_ref[1] = pull_ref[1] + tau * (b2 * t0 - b0 * t2)
            out_ref[2] = pull_ref[2] + tau * (b0 * t1 - b1 * t0)
        else:
            out_ref[...] = tau
        for write in writes:
            write.wait()

    operands = [me, *parts, table, cells, factor, source]
    if adds:
        operands += list(before)
    if last:
        operands.append(pull)
    scratch = [pltpu.VMEM((cell_total, length), jnp.float32), pltpu.SemaphoreType.DMA((steps,))]
    return pl.pallas_call(
        kernel,
        in_specs=[whole(pltpu.SMEM)] + [whole()] * (len(operands) - 1) + anywhere(len(after)),
        out_specs=(anywhere(1) if last else [whole()]) + [whole()],
        out_shape=[
            jax.ShapeDtypeStruct((cell_total, length), jnp.float32),
            jax.ShapeDtypeStruct((3, blocks, width) if last else (blocks, width), jnp.float32),
        ],
        scratch_shapes=scratch if last else [],
        compiler_params=params(),
        cost_estimate=counted(cost),
        name="z_backward",
    )(*operands, *after)


def join_rows(low, own, high, after, cost):
    rows = own.shape[0]

    def kernel(low_ref, own_ref, high_ref, after_ref, out_ref):
        out_ref[0:rows] = low_ref[...]
        out_ref[rows : 2 * rows] = own_ref[...]
        out_ref[2 * rows :] = high_ref[...]

    return pl.pallas_call(
        kernel,
        in_specs=[whole()] * 3 + anywhere(1),
        out_specs=whole(),
        out_shape=jax.ShapeDtypeStruct((3 * rows,) + own.shape[1:], jnp.float32),
        compiler_params=params(),
        cost_estimate=counted(cost),
        name="join_rows",
    )(low, own, high, after)


def spread_rows(source, after, cost):
    rows, blocks, width = source.shape

    def kernel(source_ref, *refs):
        near = refs[-1]
        spread_row = lax.broadcasted_iota(jnp.int32, (3 * rows, rows * width), 0) % rows
        spread_col = lax.broadcasted_iota(jnp.int32, (3 * rows, rows * width), 1) // width
        spread = (spread_row == spread_col).astype(jnp.bfloat16)
        for b in range(blocks):
            own = jnp.concatenate([source_ref[k, b : b + 1, :] for k in range(rows)], axis=0)
            high = own.astype(jnp.bfloat16).astype(jnp.float32)
            rest = own - high
            middle = rest.astype(jnp.bfloat16).astype(jnp.float32)
            split = jnp.concatenate([high, middle, rest - middle], axis=0).astype(jnp.bfloat16)
            near[b * width : (b + 1) * width, :] = lax.dot_general(
                split, spread, (((0,), (0,)), ((), ())), preferred_element_type=jnp.float32
            )

    return pl.pallas_call(
        kernel,
        in_specs=[whole()] + anywhere(len(after)),
        out_specs=whole(),
        out_shape=jax.ShapeDtypeStruct((blocks * width, rows * width), jnp.float32),
        compiler_params=params(),
        cost_estimate=counted(cost),
        name="spread_rows",
    )(source, *after)


def gather_rows(trios, me, plane_x, plane_y, cost):
    blocks, width = trios[0].shape[1:]
    rows = trios[0].shape[0] // 3
    stride = rows * blocks
    padded = (9 * blocks + 127) // 128 * 128

    def kernel(me_ref, *refs):
        trio_refs = refs[:3]
        far, marks, flags = refs[3:]
        toward = jnp.where(me_ref[0] & 1 == 1, -float(plane_y), float(plane_y))
        flags[...] = jnp.zeros_like(flags)
        for slot in range(3):
            for p in range(3):
                base = slot * 3 + p
                trio = trio_refs[slot]
                for k in range(rows):
                    value = trio[p * rows + k]
                    if k == 0 and p != 1:
                        value = value + float((p - 1) * plane_x)
                    if k == 1 and slot > 0:
                        value = value + (toward if slot == 1 else -toward)
                    at = base * stride + k * blocks
                    far[at : at + blocks, :] = value
                size = jnp.maximum(
                    jnp.maximum(jnp.abs(trio[p * rows + 3]), jnp.abs(trio[p * rows + 4])),
                    jnp.abs(trio[p * rows + 5]),
                )
                flags[base * blocks : (base + 1) * blocks, :] = (size > 0.0).astype(jnp.float32)
        marks[...] = lax.dot_general(
            jnp.ones((8, width), jnp.bfloat16),
            flags[...].astype(jnp.bfloat16),
            (((1,), (1,)), ((), ())),
            preferred_element_type=jnp.float32,
        ).astype(jnp.int32)

    return pl.pallas_call(
        kernel,
        in_specs=[whole(pltpu.SMEM)] + [whole()] * 3,
        out_specs=[whole()] * 2,
        out_shape=[
            jax.ShapeDtypeStruct((9 * stride, width), jnp.float32),
            jax.ShapeDtypeStruct((8, padded), jnp.int32),
        ],
        scratch_shapes=[pltpu.VMEM((padded, width), jnp.float32)],
        compiler_params=params(),
        cost_estimate=counted(cost),
        name="gather_rows",
    )(me, *trios)


def pair_pull(near, far, marks, pairs, first_block, count, after, cost):
    blocks, partners = pairs.shape
    width = near.shape[0] // blocks
    rows = near.shape[1] // width
    stride = rows * blocks

    def kernel(pairs_ref, marks_ref, near, far, *refs):
        out_ref, total = refs[-2:]
        total[...] = jnp.zeros_like(total)

        def one_block(index, carry):
            b = first_block + index
            own_at = pl.multiple_of(b * width, width)
            sum_at = pl.multiple_of(index * width, width)

            def one_partner(p, carry):
                number = pairs_ref[b, p]

                @pl.when(marks_ref[0, number] > 0)
                def _():
                    first = number // blocks * stride + number % blocks
                    other = [
                        jnp.broadcast_to(far[pl.ds(first + k * blocks, 1), :], (8, width)) for k in range(rows)
                    ]
                    for t in range(0, width, 8):
                        at = pl.ds(pl.multiple_of(own_at + t, 8), 8)
                        mine = [near[at, k * width : (k + 1) * width] for k in range(rows)]
                        dx, dy, dz = (mine[k] - other[k] for k in range(3))
                        inverse = lax.rsqrt(dx * dx + dy * dy + dz * dz + core_sq)
                        squared = inverse * inverse
                        burg_dot = mine[3] * other[3] + mine[4] * other[4] + mine[5] * other[5]
                        line_dot = mine[6] * other[6] + mine[7] * other[7] + mine[8] * other[8]
                        burg_own = mine[3] * dx + mine[4] * dy + mine[5] * dz
                        burg_far = other[3] * dx + other[4] * dy + other[5] * dz
                        weight = (line_dot * (squared * inverse)) * (
                            burg_dot - (3.0 * squared) * (burg_own * burg_far)
                        )
                        to = pl.ds(pl.multiple_of(sum_at + t, 8), 8)
                        total[0, to, :] += weight * dx
                        total[1, to, :] += weight * dy
                        total[2, to, :] += weight * dz

                return carry

            return lax.fori_loop(0, partners, one_partner, carry)

        lax.fori_loop(0, count, one_block, 0)
        ones = jnp.ones((8, width), jnp.bfloat16)
        dims = (((1,), (1,)), ((), ()))
        for k in range(3):
            high, low = halves(total[k])
            summed = lax.dot_general(ones, high, dims, preferred_element_type=jnp.float32) + lax.dot_general(
                ones, low, dims, preferred_element_type=jnp.float32
            )
            for b in range(count):
                out_ref[k, b : b + 1, :] = pair_scale * summed[0:1, b * width : (b + 1) * width]

    return pl.pallas_call(
        kernel,
        in_specs=[whole(pltpu.SMEM)] * 2 + [whole()] * 2 + anywhere(len(after)),
        out_specs=whole(),
        out_shape=jax.ShapeDtypeStruct((3, count, width), jnp.float32),
        scratch_shapes=[pltpu.VMEM((3, count * width, width), jnp.float32)],
        compiler_params=params(),
        cost_estimate=counted(cost),
        name="pair_pull",
    )(pairs, marks, near, far, *after)


def hint(name, index):
    costs = COSTS.get(name, ())
    return costs[index] if index < len(costs) else 0.0


def per_device(eigen, seg_vec, seg_off, seg_cell, blk_count, pair_list):
    plane_x, plane_y, length = eigen.shape
    groups_x = lax.axis_size("gx")
    groups_y = lax.axis_size("gy")
    per = length // groups_y
    sizes = CHUNKS if sum(CHUNKS) == per else (per,)
    offsets = [sum(sizes[:c]) for c in range(len(sizes))]
    chunks = len(sizes)
    place_x = lax.axis_index("gx").astype(jnp.int32)
    place_y = lax.axis_index("gy").astype(jnp.int32)
    me = jnp.stack([place_y, place_x])
    table = jnp.asarray(hartley_table(length))
    lines = jnp.asarray(line_tables(length, plane_x))

    def swap(parts):
        return [parts[0]] + [
            lax.ppermute(parts[d], "gy", [(i, i ^ d) for i in range(groups_y)])
            for d in range(1, groups_y)
        ]

    field = eigen.reshape(plane_x * plane_y, length)
    sent = [z_forward(field, table, me, groups_y, 0, sizes[0], [], hint("z_forward", 0))]

    seg_total = seg_cell.shape[2]
    block_total = blk_count.shape[2]
    width = seg_total // block_total
    cells = seg_cell.reshape(block_total, width)
    source, pairs = segment_rows(
        seg_vec.reshape(6, block_total, width),
        seg_off.reshape(3, block_total, width),
        cells,
        blk_count.reshape(block_total),
        pair_list.reshape(block_total, pair_list.shape[3]),
        me,
        plane_y,
        length,
        sent[0][0],
        hint("segment_rows", 0),
    )
    for c in range(1, chunks):
        sent.append(z_forward(field, table, me, groups_y, offsets[c], sizes[c], [source], hint("z_forward", c)))
    arrived = [swap(parts) for parts in sent]
    low = lax.ppermute(source, "gx", [(i, (i + 1) % groups_x) for i in range(groups_x)])
    high = lax.ppermute(source, "gx", [((i + 1) % groups_x, i) for i in range(groups_x)])

    near = spread_rows(source, [sent[-1][0]] if "near" in ORDER else [], hint("spread_rows", 0))
    flat_cells = seg_cell.reshape(1, seg_total)
    factors = sample_factors(flat_cells, table, me, groups_y, offsets, sizes, 0.0)

    levels = groups_x.bit_length() - 1
    forward, others, joined = [], [], []
    for c in range(chunks):
        after = [low, high, near, factors[0]] if c == 0 else [joined[0][-1] if "yf1" in ORDER else forward[-1][1]]
        forward.append(y_forward(arrived[c], table, lines, me, offsets[c], sizes[c], plane_x, plane_y, after, hint("y_forward", c)))
        others.append([])
        joined.append([forward[c][1]])
        for level in range(levels):
            others[c].append(lax.ppermute(joined[c][-1], "gx", [(i, i ^ 2**level) for i in range(groups_x)]))
            if level < levels - 1:
                joined[c].append(
                    join_ends(joined[c][-1], others[c][-1], forward[c][2], me, level, plane_x, [], hint("join_ends", 2 * c + level))
                )
    trio = join_rows(low, source, high, joined[0][-1] if "trio" in ORDER else forward[-1][1], hint("join_rows", 0))
    other = [(i, (i + 1 if i % 2 else i - 1) % groups_y) for i in range(groups_y)]
    trios = [
        trio,
        lax.ppermute(trio, "gy", [(i, i ^ 1) for i in range(groups_y)]),
        lax.ppermute(trio, "gy", other),
    ]
    far, marks = gather_rows(trios, me, plane_x, plane_y, hint("gather_rows", 0))

    shares = SHARES if len(SHARES) == chunks and sum(SHARES) == block_total else (0,) * (chunks - 1) + (block_total,)
    returned, pulls = [], []
    for c in range(chunks):
        spec, ends, own_lines = forward[c]
        after = pulls[-1:] if pulls else [far] + (joined[-1][-1:] if "yb0" in ORDER else [])
        returned.append(y_backward(spec, ends, others[c], table, own_lines, me, groups_y, plane_y, after, hint("y_backward", c)))
        first = sum(shares[:c])
        if shares[c]:
            pulls.append(pair_pull(near, far, marks, pairs, first, shares[c], returned[-1][:1], hint("pair_pull", c)))
    landed = [swap(parts) for parts in returned]

    pull = pulls[0] if len(pulls) == 1 else jnp.concatenate(pulls, axis=1)
    before = None
    for c in range(chunks):
        before = z_backward(
            landed[c], table, flat_cells, factors[c], me, groups_y, offsets[c], sizes[c], before,
            pull if c == chunks - 1 else None, source, pulls[-1:], hint("z_backward", c),
        )
    stress, force = before
    return stress.reshape(eigen.shape), force.reshape(3, 1, 1, seg_total)


def solution(mesh):
    return jax.shard_map(
        per_device,
        mesh=mesh,
        in_specs=(
            P("gx", "gy", None),
            P(None, "gx", "gy", None),
            P(None, "gx", "gy", None),
            P("gx", "gy", None),
            P("gx", "gy", None),
            P("gx", "gy", None, None),
        ),
        out_specs=(P("gx", "gy", None), P(None, "gx", "gy", None)),
        check_vma=False,
    )
```
